128 devices in a mesh: ctx: 16 (over y, x_hi, core), fsdp: 8 (over z, x_lo).
Axes of the slice: x: 4 (x_hi: 2, x_lo: 2; x = x_hi * 2 + x_lo), y: 4, z: 4, core: 2. Of those that a mesh axis runs over, the one named last changes fastest.
Arguments:
- inputs: bfloat16 [8, 2048, 1024], P('fsdp', 'ctx'), may hold values from -4 to 4, as said below
- w_query: bfloat16 [1024, 1024], P('fsdp'), may hold values from -0.176776695 to 0.176776695, as said below
- b_query: bfloat16 [1024], P('fsdp'), may hold values from -4 to 4
- w_key: bfloat16 [1024, 1024], P('fsdp'), may hold values from -0.176776695 to 0.176776695, as said below
- w_value: bfloat16 [1024, 1024], P('fsdp'), may hold values from -0.1875 to 0.1875
- b_value: bfloat16 [1024], P('fsdp'), may hold values from -4 to 4
- w_out: bfloat16 [1024, 1024], P('fsdp'), may hold values from -6 to 6
- b_out: bfloat16 [1024], P('fsdp'), may hold values from -4 to 4
- gain_one: bfloat16 [1024], P('fsdp'), may hold values from 0.5 to 1.5
- shift_one: bfloat16 [1024], P('fsdp'), may hold values from -4 to 4
- w_up: bfloat16 [1024, 4096], P('fsdp'), may hold values from -0.1875 to 0.1875
- b_up: bfloat16 [4096], P('fsdp'), may hold values from -4 to 4
- w_down: bfloat16 [4096, 1024], P('fsdp'), may hold values from -0.125 to 0.125
- b_down: bfloat16 [1024], P('fsdp'), may hold values from -4 to 4
- gain_two: bfloat16 [1024], P('fsdp'), may hold values from 0.5 to 1.5
- shift_two: bfloat16 [1024], P('fsdp'), may hold values from -4 to 4
- cotangent: bfloat16 [8, 2048, 1024], P('fsdp', 'ctx'), may hold values from -6 to 6
Outputs:
- output: bfloat16 [8, 2048, 1024], P('fsdp', 'ctx')
- grad_inputs: float32 [8, 2048, 1024], P('fsdp', 'ctx')
- grad_w_query: float32 [1024, 1024], P('fsdp')
- grad_b_query: float32 [1024], P('fsdp')
- grad_w_key: float32 [1024, 1024], P('fsdp')
- grad_w_value: float32 [1024, 1024], P('fsdp')
- grad_b_value: float32 [1024], P('fsdp')
- grad_w_out: float32 [1024, 1024], P('fsdp')
- grad_b_out: float32 [1024], P('fsdp')
- grad_gain_one: float32 [1024], P('fsdp')
- grad_shift_one: float32 [1024], P('fsdp')
- grad_w_up: float32 [1024, 4096], P('fsdp')
- grad_b_up: float32 [4096], P('fsdp')
- grad_w_down: float32 [4096, 1024], P('fsdp')
- grad_b_down: float32 [1024], P('fsdp')
- grad_gain_two: float32 [1024], P('fsdp')
- grad_shift_two: float32 [1024], P('fsdp')
The draws below stay inside these ranges and needn't reach their ends.
Inputs may be any that keep to these rules, and one draw needn't show every extreme that they name: `inputs`: independent entries of mean 0 and deviation 1. `w_query`: independent entries of mean 0 and deviation (D // 2) ** -0.5. `w_key`: independent entries of mean 0 and deviation (D // 2) ** -0.5.
All inputs are finite; a program needn't handle non-finite values.
Results may differ from the reference program's by a relative error of at most 0.024.
Values may be sent and summed in bfloat16 or wider, within the bound.
No kernel may reach another device: no remote copies, remote signals or barrier semaphores. Data moves between devices by JAX's collectives and lax.ppermute only.
A program may use at most 192 MiB of HBM per device.

```python
import jax
import jax.numpy as jnp
from jax import lax

D = 1024
FF = 4096
HEADS = 16
HEAD_DIM = 64
LENGTH = 2048
SEQS = 8


def level_field(key, shape, deviation):
    values = jax.random.normal(key, shape, jnp.float32) * deviation
    return jnp.clip(values, -4.0 * deviation, 4.0 * deviation)


def draw_inputs(key, part):
    key = jax.random.fold_in(key, 11)
    return level_field(key, (SEQS, LENGTH, D), 1.0).astype(jnp.bfloat16)


def draw_w_query(key, part):
    key = jax.random.fold_in(key, 23)
    return level_field(key, (D, D), (D // 2) ** (-0.5)).astype(jnp.bfloat16)


def draw_w_key(key, part):
    key = jax.random.fold_in(key, 37)
    return level_field(key, (D, D), (D // 2) ** (-0.5)).astype(jnp.bfloat16)


def block_scale(rng, dims, split, low, largest):
    level, own = 1.0, jax.random.fold_in(rng, 6)
    for axis_at, shards_of in split:
        draws = jnp.exp(jax.random.uniform(jax.random.fold_in(own, axis_at), (shards_of,), jnp.float32, low / len(split), largest / len(split)))
        level = level * jnp.repeat(draws, dims[axis_at] // shards_of).reshape([-1 if axis == axis_at else 1 for axis in range(len(dims))])
    return level


def gaussian(stream_key, extent, scale, most, shards=(), held_as=jnp.bfloat16):
    array = jax.random.normal(stream_key, extent, jnp.float32) * scale
    if len(shards) > 0:
        array = block_scale(stream_key, extent, shards, -0.22, 0.18) * array
    return jnp.clip(array, min=-most, max=most).astype(held_as)


def setup_inputs(seed: int = 0) -> dict:
    key_list = jax.random.split(jax.random.key(seed), 18)
    return {
        "inputs": draw_inputs(jax.random.fold_in(key_list[17], 71), 0),
        "w_query": draw_w_query(jax.random.fold_in(key_list[17], 71), 0),
        "b_query": gaussian(key_list[2], (D,), 0.3, 4.0, ((0, 8),)),
        "w_key": draw_w_key(jax.random.fold_in(key_list[17], 71), 0),
        "w_value": gaussian(key_list[4], (D, D), D ** -0.5, 0.1875, ((0, 8),)),
        "b_value": gaussian(key_list[5], (D,), 0.3, 4.0, ((0, 8),)),
        "w_out": gaussian(key_list[6], (D, D), (max(1, 2 * D // LENGTH)) ** -0.5, 6.0, ((0, 8),)),
        "b_out": gaussian(key_list[7], (D,), 0.3, 4.0, ((0, 8),)),
        "gain_one": jnp.clip(1.0 + 0.1 * jax.random.normal(key_list[8], (D,), jnp.float32), 0.5, 1.5).astype(jnp.bfloat16),
        "shift_one": gaussian(key_list[9], (D,), 0.3, 4.0, ((0, 8),)),
        "w_up": gaussian(key_list[10], (D, FF), D ** -0.5, 0.1875, ((0, 8),)),
        "b_up": gaussian(key_list[11], (FF,), 0.3, 4.0, ((0, 8),)),
        "w_down": gaussian(key_list[12], (FF, D), (FF // 2) ** -0.5, 0.125, ((0, 8),)),
        "b_down": gaussian(key_list[13], (D,), 0.3, 4.0, ((0, 8),)),
        "gain_two": jnp.clip(1.0 + 0.1 * jax.random.normal(key_list[14], (D,), jnp.float32), 0.5, 1.5).astype(jnp.bfloat16),
        "shift_two": gaussian(key_list[15], (D,), 0.3, 4.0, ((0, 8),)),
        "cotangent": gaussian(key_list[16], (SEQS, LENGTH, D), 1.0, 6.0, ((0, 8), (1, 16))),
    }


@jax.custom_vjp
def low(v):
    return lax.optimization_barrier(v.astype(jnp.bfloat16)).astype(jnp.float32)

@jax.custom_vjp
def low_back(v):
    return v

def low_keep(v):
    return (low(v), None)

def low_pass(kept, grad):
    return (grad,)

def back_keep(v):
    return (v, None)

def back_low(kept, grad):
    return (low(grad),)
low.defvjp(low_keep, low_pass)
low_back.defvjp(back_keep, back_low)
EPSILON = 1e-05
EXACT = lax.Precision.HIGHEST

def rounded(value):
    return low(low_back(value))

def product(matrix, other):
    return jnp.dot(matrix, other, precision=EXACT)

def norm_rows(hidden, gain, shift):
    center = hidden - lax.optimization_barrier(jnp.mean(hidden, axis=-1, keepdims=True))
    spread = lax.optimization_barrier(jnp.mean(center * center, axis=-1, keepdims=True))
    return center * lax.rsqrt(spread + EPSILON) * gain + shift

def attend_sequence(triple):
    query_seq, key_seq, value_seq = triple
    scores = low_back(jnp.einsum('qhe,khe->hqk', query_seq, key_seq, precision=EXACT))
    chances = low(jax.nn.softmax(scores, axis=-1))
    return jnp.einsum('hqk,khe->qhe', chances, value_seq, precision=EXACT)

def forward(params):
    inputs, w_query, b_query, w_key, w_value, b_value, w_out, b_out, gain_one, shift_one, w_up, b_up, w_down, b_down, gain_two, shift_two = params
    tok_rows = inputs.reshape(SEQS * LENGTH, D)
    scaling = HEAD_DIM ** (-0.5)
    query_rows = rounded((product(tok_rows, w_query) + b_query) * scaling)
    key_rows = rounded(product(tok_rows, w_key))
    value_rows = rounded(product(tok_rows, w_value) + b_value)
    split_shape = (SEQS, LENGTH, HEADS, HEAD_DIM)
    mixed = lax.map(jax.checkpoint(attend_sequence), (query_rows.reshape(split_shape), key_rows.reshape(split_shape), value_rows.reshape(split_shape)))
    context = rounded(mixed.reshape(SEQS * LENGTH, D))
    branch = low_back(product(context, w_out) + b_out)
    first = norm_rows(tok_rows + branch, gain_one, shift_one)
    hidden = low_back(product(low(first), w_up) + b_up)
    active = low(jax.nn.gelu(hidden, approximate=False))
    second = low_back(product(active, w_down) + b_down)
    return norm_rows(first + second, gain_two, shift_two).reshape(SEQS, LENGTH, D)

def reference(inputs, w_query, b_query, w_key, w_value, b_value, w_out, b_out, gain_one, shift_one, w_up, b_up, w_down, b_down, gain_two, shift_two, cotangent):
    params = (inputs, w_query, b_query, w_key, w_value, b_value, w_out, b_out, gain_one, shift_one, w_up, b_up, w_down, b_down, gain_two, shift_two)
    floats = tuple((element.astype(jnp.float32) for element in params))
    output, pullback = jax.vjp(forward, floats)
    grads = pullback(cotangent.astype(jnp.float32))[0]
    return (output.astype(jnp.bfloat16), grads[0], grads[1], grads[2], grads[3], grads[4], grads[5], grads[6], grads[7], grads[8], grads[9], grads[10], grads[11], grads[12], grads[13], grads[14], grads[15])
```

```python
import functools

import jax
import jax.numpy as jnp
from jax import lax
from jax.experimental import pallas as pl
from jax.experimental.pallas import tpu as pltpu
from jax.sharding import PartitionSpec as P

EPSILON = 1e-05
LOW = jnp.bfloat16
F32 = jnp.float32
WIDTH = 1024
HEAD = 64
ROWS = 128
LENGTH = 2048
CHUNK = 512
QUERIES = 256
SAME_CORE = [list(range(0, 16, 2)), list(range(1, 16, 2))]
SAME_LOW = [list(range(0, 8, 2)), list(range(1, 8, 2))]
VMEM_LIMIT = 50 * 1024 * 1024


def over_ctx(block, y=0, x=0, core=0):
    route = [
        (i, (((i >> 2) + y) % 4) * 4 + (((i >> 1) & 1) ^ x) * 2 + ((i & 1) ^ core))
        for i in range(16)
    ]
    return lax.ppermute(block, "ctx", route)


def over_fsdp(block, z=0, x=0):
    route = [(i, (((i >> 1) + z) % 4) * 2 + ((i & 1) ^ x)) for i in range(8)]
    return lax.ppermute(block, "fsdp", route)


def dims(matrix, other, left, right):
    return lax.dot_general(
        matrix, other, (((left,), (right,)), ((), ())), preferred_element_type=F32
    )


def dot(matrix, other):
    return dims(matrix, other, 1, 0)


def split_low(value):
    high = value.astype(LOW)
    return high, (value - high.astype(F32)).astype(LOW)


def norm_forward(hidden, gain, shift):
    center = hidden - jnp.mean(hidden, axis=-1, keepdims=True)
    scale = lax.rsqrt(jnp.mean(center * center, axis=-1, keepdims=True) + EPSILON)
    unit = center * scale
    return unit * gain + shift, unit, scale


def norm_backward(grad, unit, scale, gain):
    inner = grad * gain
    mean_inner = jnp.mean(inner, axis=-1, keepdims=True)
    mean_unit = jnp.mean(inner * unit, axis=-1, keepdims=True)
    back = scale * (inner - mean_inner - unit * mean_unit)
    return back, jnp.sum(grad * unit, axis=0), jnp.sum(grad, axis=0)


def forward_kernel(order, *refs):
    parts = refs[:8]
    w_ref, bias_q, bias_v, qkv, rows, mixed_low, mixed, total, held = refs[8:]
    weight = jnp.concatenate([w_ref[f, : 3 * HEAD, :] for f in range(8)], axis=1)
    for index, part in enumerate(parts):
        span = slice(index * QUERIES, (index + 1) * QUERIES)
        product = dims(weight, part[...], 1, 1)
        query = (product[:HEAD] + bias_q[...]) * (HEAD**-0.5)
        value = product[2 * HEAD :] + bias_v[...]
        pair = jnp.concatenate([product[HEAD : 2 * HEAD], value], axis=0)
        qkv[:HEAD, span] = query.astype(LOW)
        qkv[HEAD:, span] = pair.astype(LOW)
        rows[span, :] = pair.T.astype(LOW)

    def step(index, carry):
        span = pl.ds(pl.multiple_of(index * QUERIES, QUERIES), QUERIES)
        query = qkv[:HEAD, span]
        padded = jnp.concatenate([query, jnp.zeros_like(query)], axis=0)
        peak = None
        for at in range(0, LENGTH, CHUNK):
            scores = dot(rows[at : at + CHUNK, :], padded)
            held[at : at + CHUNK, :] = scores
            top = jnp.max(scores, axis=0, keepdims=True)
            peak = top if peak is None else jnp.maximum(peak, top)
        weight_sum = jnp.zeros((1, QUERIES), F32)
        acc = jnp.zeros((HEAD, QUERIES), F32)
        for at in range(0, LENGTH, CHUNK):
            weights = jnp.exp(held[at : at + CHUNK, :] - peak)
            weight_sum += jnp.sum(weights, axis=0, keepdims=True)
            acc += dot(qkv[2 * HEAD :, at : at + CHUNK], weights.astype(LOW))
        acc = acc / weight_sum
        mixed[:, span] = acc
        total[:, span] = peak + jnp.log(weight_sum)
        mixed_low[order[2 * index]] = acc[:, :ROWS].astype(LOW)
        mixed_low[order[2 * index + 1]] = acc[:, ROWS:].astype(LOW)
        return carry

    lax.fori_loop(0, LENGTH // QUERIES, step, 0)


def backward_kernel(order, grad_ref, qkv, rows, mixed, total, sent, kept, key_acc, value_acc):
    key_acc[...] = jnp.zeros_like(key_acc)
    value_acc[...] = jnp.zeros_like(value_acc)

    def step(index, carry):
        span = pl.ds(pl.multiple_of(index * QUERIES, QUERIES), QUERIES)
        first, second = order[2 * index], order[2 * index + 1]
        query = qkv[:HEAD, span]
        grad = jnp.concatenate([grad_ref[first], grad_ref[second]], axis=1)
        delta = jnp.sum(grad.astype(F32) * mixed[:, span], axis=0, keepdims=True)
        log_total = total[:, span]
        query_pad = jnp.concatenate([query, jnp.zeros_like(query)], axis=0)
        grad_pad = jnp.concatenate([jnp.zeros_like(grad), grad], axis=0)
        query_grad = jnp.zeros((HEAD, QUERIES), F32)
        for at in range(0, LENGTH, CHUNK):
            block = rows[at : at + CHUNK, :]
            chances = jnp.exp(dot(block, query_pad) - log_total)
            chance_grad = dot(block, grad_pad)
            score_grad = (chances * (chance_grad - delta)).astype(LOW)
            value_acc[:, at : at + CHUNK] += dims(grad, chances.astype(LOW), 1, 1)
            key_acc[:, at : at + CHUNK] += dims(query, score_grad, 1, 1)
            query_grad += dot(qkv[HEAD : 2 * HEAD, at : at + CHUNK], score_grad)
        low = query_grad.astype(LOW)
        kept[:HEAD, span] = low
        sent[first, :HEAD, :] = low[:, :ROWS]
        sent[second, :HEAD, :] = low[:, ROWS:]
        return carry

    lax.fori_loop(0, LENGTH // QUERIES, step, 0)
    kept[HEAD : 2 * HEAD, :] = key_acc[...].astype(LOW)
    kept[2 * HEAD :, :] = value_acc[...].astype(LOW)
    for index in range(LENGTH // ROWS):
        sent[order[index], HEAD:, :] = kept[HEAD:, index * ROWS : (index + 1) * ROWS]


def projection_kernel(grads, *refs):
    parts, out = refs[:8], refs[8]
    acc = None
    for index, part in enumerate(parts):
        term = dot(grads[:, index * QUERIES : (index + 1) * QUERIES], part[...])
        acc = term if acc is None else acc + term
    sums = dims(jnp.ones((8, LENGTH), LOW), grads[...], 1, 1)[:1]
    sums = jnp.concatenate([sums, jnp.zeros((1, HEAD), F32)], axis=1)
    high, rest = split_low(sums)
    tail = jnp.concatenate(
        [
            high.astype(F32)[:, :ROWS],
            high.astype(F32)[:, ROWS:],
            rest.astype(F32)[:, :ROWS],
            rest.astype(F32)[:, ROWS:],
            jnp.zeros((12, ROWS), F32),
        ],
        axis=0,
    ).astype(LOW)
    for index in range(8):
        out[index, : 3 * HEAD, :] = acc[:, index * ROWS : (index + 1) * ROWS].astype(LOW)
        out[index, 3 * HEAD :, :] = tail


def call(kernel, outs, scratch, flops, moved, *operands):
    in_specs = [pl.BlockSpec(memory_space=pltpu.SMEM if operand.dtype == jnp.int32 else pltpu.VMEM) for operand in operands]
    return pl.pallas_call(
        kernel,
        out_shape=[jax.ShapeDtypeStruct(shape, dtype) for shape, dtype in outs],
        in_specs=in_specs,
        out_specs=[pl.BlockSpec(memory_space=pltpu.VMEM)] * len(outs),
        scratch_shapes=scratch,
        compiler_params=pltpu.CompilerParams(vmem_limit_bytes=VMEM_LIMIT),
        cost_estimate=pl.CostEstimate(flops=flops, bytes_accessed=moved, transcendentals=0),
    )(*operands)


def on_device(
    inputs,
    w_query,
    b_query,
    w_key,
    w_value,
    b_value,
    w_out,
    b_out,
    gain_one,
    shift_one,
    w_up,
    b_up,
    w_down,
    b_down,
    gain_two,
    shift_two,
    cotangent,
):
    ctx, fsdp = lax.axis_index("ctx"), lax.axis_index("fsdp")
    core, x_hi, y = ctx & 1, (ctx >> 1) & 1, ctx >> 2
    x_lo, z = fsdp & 1, fsdp >> 1

    own = inputs.reshape(ROWS, WIDTH)
    pair = jnp.concatenate([own, over_ctx(own, x=1)], axis=0)
    near = [pair] + [over_ctx(pair, y=k) for k in (1, 2, 3)]
    parts = near + [over_ctx(part, core=1) for part in near]
    order = jnp.stack(
        [
            ((y - k) % 4) * 4 + (x_hi ^ j) * 2 + (core ^ s)
            for s in range(2)
            for k in range(4)
            for j in range(2)
        ]
    ).astype(jnp.int32)

    columns = [
        lax.dynamic_slice(w, (0, ctx * HEAD), (ROWS, HEAD)).T for w in (w_query, w_key, w_value)
    ]
    vectors = jnp.concatenate(
        [
            jnp.stack([b_query, b_value, b_out, gain_one, shift_one, b_down, gain_two, shift_two]),
            b_up.reshape(4, ROWS),
            jnp.zeros((4, ROWS), LOW),
        ]
    )
    message = jnp.concatenate(columns + [vectors], axis=0)
    heads = lax.all_to_all(
        jnp.broadcast_to(message[None], (8,) + message.shape), "fsdp", 0, 0, tiled=True
    )
    vecs = heads[:, 3 * HEAD :, :].astype(F32)

    def whole(index):
        return vecs[:, index, :].reshape(WIDTH)

    vec_query, vec_value, vec_out, gain_a, shift_a, vec_down, gain_b, shift_b = (
        whole(index) for index in range(8)
    )
    vec_up = lax.dynamic_slice(
        vecs[:, 8:12, :].reshape(8, 512), (0, core * 256), (8, 256)
    ).reshape(2048)
    bias_q = lax.dynamic_slice(vec_query, (ctx * HEAD,), (HEAD,)).reshape(HEAD, 1)
    bias_v = lax.dynamic_slice(vec_value, (ctx * HEAD,), (HEAD,)).reshape(HEAD, 1)

    half_out = lax.dynamic_slice(w_out, (core * 64, 0), (64, WIDTH))
    half_up = lax.dynamic_slice(
        w_up.reshape(ROWS, 8, 512), (0, 0, core * 256), (ROWS, 8, 256)
    ).reshape(ROWS, 2048)
    half_down = lax.dynamic_slice(w_down, (core * 256, 0), (256, WIDTH))
    half_in = [lax.dynamic_slice(w, (core * 64, 0), (64, WIDTH)) for w in (w_query, w_key, w_value)]
    packed = jnp.concatenate([half_out, half_up[:, :WIDTH], half_up[:, WIDTH:], half_down], axis=0)
    packed_in = jnp.concatenate(half_in, axis=0)

    def gather(block):
        other = over_fsdp(block, x=1)
        found = [(0, 0, block), (0, 1, other)]
        for k in (1, 3, 2):
            found.append((k, 0, over_fsdp(block, z=k)))
            found.append((k, 1, over_fsdp(other, z=k)))
        return [(((z - k) % 4) * 2 + (x_lo ^ j), part) for k, j, part in found]

    def place(found, low, high):
        size = high - low
        held = jnp.zeros((8, size, WIDTH), LOW)
        for at, part in found:
            held = lax.dynamic_update_slice(held, part[None, low:high], (at, 0, 0))
        return held

    found = gather(packed)
    mat_out = place(found, 0, 64)
    up_left = place(found, 64, 192).reshape(WIDTH, WIDTH)
    up_right = place(found, 192, 320).reshape(WIDTH, WIDTH)
    mat_down = place(found, 320, 576).reshape(2048, WIDTH)
    found_in = gather(packed_in)
    mat_in = place(found_in, 0, 192)

    def both_halves(mine):
        theirs = over_ctx(mine, core=1)
        return jnp.where(core == 0, mine, theirs), jnp.where(core == 0, theirs, mine)

    mat_out = jnp.stack(both_halves(mat_out), axis=1).reshape(WIDTH, WIDTH)
    mat_in = jnp.stack(both_halves(mat_in.reshape(8, 3, 64, WIDTH)), axis=2)
    mat_query, mat_key, mat_value = (mat_in[:, i].reshape(WIDTH, WIDTH) for i in range(3))

    qkv, rows, mixed_low, mixed, total = call(
        forward_kernel,
        [
            ((3 * HEAD, LENGTH), LOW),
            ((LENGTH, 2 * HEAD), LOW),
            ((16, HEAD, ROWS), LOW),
            ((HEAD, LENGTH), F32),
            ((1, LENGTH), F32),
        ],
        [pltpu.VMEM((LENGTH, QUERIES), F32)],
        10**10,
        10**7,
        order,
        *parts,
        heads,
        bias_q,
        bias_v,
    )
    context = lax.all_to_all(mixed_low, "ctx", 0, 0, tiled=True).reshape(WIDTH, ROWS)
    branch = dims(context, mat_out, 0, 0) + vec_out
    first, unit_one, scale_one = norm_forward(own.astype(F32) + branch, gain_a, shift_a)
    first_low = first.astype(LOW)
    first_two = jnp.concatenate([first_low, over_ctx(first_low, core=1)], axis=0)
    hidden = jnp.concatenate([dot(first_two, up_left), dot(first_two, up_right)], axis=1) + vec_up
    gate = 0.5 * (1.0 + lax.erf(hidden * (0.5**0.5)))
    slope = gate + hidden * jnp.exp(-0.5 * hidden * hidden) * 0.3989422804014327
    active = (hidden * gate).astype(LOW)
    second = dot(active, mat_down)
    second = second[:ROWS] + over_ctx(second[ROWS:], core=1) + vec_down
    result, unit_two, scale_two = norm_forward(first + second, gain_b, shift_b)

    grad_out = cotangent.reshape(ROWS, WIDTH).astype(F32)
    grad_two, grad_gain_b, grad_shift_b = norm_backward(grad_out, unit_two, scale_two, gain_b)
    grad_second = grad_two.astype(LOW)
    grad_vec_down = jnp.sum(grad_second.astype(F32), axis=0)
    second_two = jnp.concatenate([grad_second, over_ctx(grad_second, core=1)], axis=0)
    grad_hidden = (slope * dims(second_two, mat_down, 1, 1)).astype(LOW)
    grad_vec_up = jnp.sum(grad_hidden.astype(F32), axis=0)
    grad_first = dims(grad_hidden[:, :WIDTH], up_left, 1, 1) + dims(
        grad_hidden[:, WIDTH:], up_right, 1, 1
    )
    grad_first = grad_two + grad_first[:ROWS] + over_ctx(grad_first[ROWS:], core=1)
    grad_one, grad_gain_a, grad_shift_a = norm_backward(grad_first, unit_one, scale_one, gain_a)
    grad_branch = grad_one.astype(LOW)
    grad_vec_out = jnp.sum(grad_branch.astype(F32), axis=0)
    grad_context = dims(mat_out, grad_branch, 1, 1).astype(LOW).reshape(16, HEAD, ROWS)
    grad_heads = lax.all_to_all(grad_context, "ctx", 0, 0, tiled=True)
    sent, kept = call(
        backward_kernel,
        [((16, 3 * HEAD, ROWS), LOW), ((3 * HEAD, LENGTH), LOW)],
        [pltpu.VMEM((HEAD, LENGTH), F32), pltpu.VMEM((HEAD, LENGTH), F32)],
        10**10,
        10**7,
        order,
        grad_heads,
        qkv,
        rows,
        mixed,
        total,
    )
    back = lax.all_to_all(sent, "ctx", 0, 0, tiled=True)
    grad_in = grad_one + (
        dims(back[:, :HEAD].reshape(WIDTH, ROWS), mat_query, 0, 1) * (HEAD**-0.5)
        + dims(back[:, HEAD : 2 * HEAD].reshape(WIDTH, ROWS), mat_key, 0, 1)
        + dims(back[:, 2 * HEAD :].reshape(WIDTH, ROWS), mat_value, 0, 1)
    )

    (pieces,) = call(
        projection_kernel, [((8, 208, ROWS), LOW)], [], 10**9, 10**7, kept, *parts
    )
    pieces = jnp.sum(lax.all_to_all(pieces, "fsdp", 0, 0, tiled=True).astype(F32), axis=0)
    sums = jnp.concatenate(split_low(pieces[192:194] + pieces[194:196]), axis=0)
    message = jnp.concatenate([pieces[:192].astype(LOW), sums, jnp.zeros((12, ROWS), LOW)], axis=0)
    shared = lax.all_to_all(
        jnp.broadcast_to(message[None], (16,) + message.shape), "ctx", 0, 0, tiled=True
    ).astype(F32)
    grad_mat_query = shared[:, :HEAD].reshape(WIDTH, ROWS).T * (HEAD**-0.5)
    grad_mat_key = shared[:, HEAD : 2 * HEAD].reshape(WIDTH, ROWS).T
    grad_mat_value = shared[:, 2 * HEAD : 3 * HEAD].reshape(WIDTH, ROWS).T
    vec_sums = shared[:, 192:194] + shared[:, 194:196]
    mine = lax.dynamic_slice(vec_sums, (fsdp * 2, 0, 0), (2, 2, ROWS))
    grad_vec_query = mine[:, 0, :HEAD].reshape(ROWS) * (HEAD**-0.5)
    grad_vec_value = mine[:, 1, :HEAD].reshape(ROWS)

    def to_quarters(block, axis):
        size = block.shape[axis] // 4

        def quarter(index):
            return lax.dynamic_slice_in_dim(block, index * size, size, axis)

        return [quarter(z)] + [over_fsdp(quarter((z + k) % 4), z=k) for k in (1, 2, 3)]

    def from_all(block):
        return [block] + [over_fsdp(block, z=k) for k in (1, 2, 3)]

    def tokens(block):
        mine = jnp.stack(from_all(block))
        return jnp.stack([mine, over_ctx(mine, core=1)], axis=1).reshape(8 * ROWS, -1)

    active_z = jnp.concatenate(to_quarters(active, 1), axis=0)
    first_z = tokens(first_low)
    second_z = tokens(grad_second)
    hidden_z = jnp.concatenate(to_quarters(grad_hidden, 1), axis=0)
    context_z = jnp.concatenate(to_quarters(context, 0), axis=1)
    branch_z = jnp.concatenate(from_all(grad_branch), axis=0)
    down = dims(active_z, second_z, 0, 0).reshape(2, 256, WIDTH)
    up = dims(first_z, hidden_z, 0, 0).reshape(4, 2, ROWS, 512)
    out = dot(context_z, branch_z).reshape(2, 2, 64, WIDTH)

    def pick(block, index, axis):
        return lax.dynamic_index_in_dim(block, index, axis, keepdims=False)

    out = pick(out, core, 1) + over_ctx(pick(out, 1 - core, 1).astype(LOW), core=1).astype(F32)

    def wide(block):
        return jnp.concatenate([block[:, :2], block[:, 2:]], axis=-1).reshape(8, 32, WIDTH)

    def bundle(index):
        rows_up = pick(up, index, 1).reshape(4, 8, 16, 512).transpose(1, 0, 2, 3)
        return jnp.concatenate(
            [
                pick(down, index, 0).reshape(8, 32, WIDTH),
                wide(rows_up),
                pick(out, index, 0).reshape(8, 8, WIDTH),
            ],
            axis=1,
        )

    summed = bundle(x_lo) + over_fsdp(bundle(1 - x_lo).astype(LOW), x=1).astype(F32)
    summed = jnp.sum(
        lax.all_to_all(
            summed.astype(LOW), "ctx", 0, 0, axis_index_groups=SAME_CORE, tiled=True
        ).astype(F32),
        axis=0,
    ).astype(LOW)
    piece = summed[32:64].reshape(2, 16, WIDTH)
    piece = jnp.concatenate([piece[:, :, :512], piece[:, :, 512:]], axis=0)
    piece = lax.all_to_all(piece, "fsdp", 0, 0, axis_index_groups=SAME_LOW, tiled=True)
    piece = jnp.concatenate([piece[:2], piece[2:]], axis=-1).reshape(32, WIDTH)
    message = jnp.concatenate([summed[:32], piece, summed[64:]], axis=0)
    shared = lax.all_to_all(
        jnp.broadcast_to(message[None], (8, 72, WIDTH)),
        "ctx",
        0,
        0,
        axis_index_groups=SAME_CORE,
        tiled=True,
    )
    shared = jnp.stack(both_halves(shared)).astype(F32)
    grad_mat_down = shared[:, :, :32].reshape(512, WIDTH)
    grad_mat_out = shared[:, :, 64:].reshape(ROWS, WIDTH)
    grad_mat_up = (
        shared[:, :, 32:64]
        .reshape(2, 8, 2, 16, 2, 2, 256)
        .transpose(1, 3, 4, 2, 5, 0, 6)
        .reshape(ROWS, 4096)
    )

    halves = jnp.zeros((8, 2, 256), F32)
    halves = lax.dynamic_update_slice(halves, grad_vec_up.reshape(8, 1, 256), (0, core, 0))
    vector_grads = jnp.concatenate(
        [
            jnp.stack(
                [grad_vec_out, grad_gain_a, grad_shift_a, grad_vec_down, grad_gain_b, grad_shift_b]
            )
            .reshape(6, 8, ROWS)
            .transpose(1, 0, 2),
            halves.reshape(8, 4, ROWS),
        ],
        axis=1,
    )
    vector_grads = lax.psum(vector_grads, ("ctx", "fsdp"))
    vector_grads = pick(vector_grads, fsdp, 0)

    return (
        result.reshape(1, ROWS, WIDTH).astype(LOW),
        grad_in.reshape(1, ROWS, WIDTH),
        grad_mat_query,
        grad_vec_query,
        grad_mat_key,
        grad_mat_value,
        grad_vec_value,
        grad_mat_out,
        vector_grads[0],
        vector_grads[1],
        vector_grads[2],
        grad_mat_up,
        vector_grads[6:10].reshape(512),
        grad_mat_down,
        vector_grads[3],
        vector_grads[4],
        vector_grads[5],
    )


def solution(mesh):
    tokens, matrix, vector = P("fsdp", "ctx", None), P("fsdp", None), P("fsdp")
    return jax.shard_map(
        on_device,
        mesh=mesh,
        in_specs=(
            tokens,
            matrix,
            vector,
            matrix,
            matrix,
            vector,
            matrix,
            vector,
            vector,
            vector,
            matrix,
            vector,
            matrix,
            vector,
            vector,
            vector,
            tokens,
        ),
        out_specs=(
            tokens,
            tokens,
            matrix,
            vector,
            matrix,
            matrix,
            vector,
            matrix,
            vector,
            vector,
            vector,
            matrix,
            vector,
            matrix,
            vector,
            vector,
            vector,
        ),
        check_vma=False,
    )
```

```python
import functools

import jax
import jax.numpy as jnp
from jax import lax
from jax.experimental import pallas as pl
from jax.experimental.pallas import tpu as pltpu
from jax.sharding import PartitionSpec as P

EPSILON = 1e-05
LOW = jnp.bfloat16
F32 = jnp.float32
WIDTH = 1024
HEAD = 64
ROWS = 128
LENGTH = 2048
CHUNK = 512
QUERIES = 256
SAME_CORE = [list(range(0, 16, 2)), list(range(1, 16, 2))]
SAME_QUARTER = [
    [(high * 2 + low) * 4 + x * 2 + core for high in range(2) for x in range(2)]
    for low in range(2)
    for core in range(2)
]
CORE, FAR_X, NEAR_Y = 1, 2, 4
VMEM_LIMIT = 50 * 1024 * 1024


def swap(block, bit):
    return lax.ppermute(block, "ctx", [(i, i ^ bit) for i in range(16)])


def along_y(block, steps):
    return lax.ppermute(block, "ctx", [(i, (i + 4 * steps) % 16) for i in range(16)])


def along_z(block, steps):
    return lax.ppermute(block, "fsdp", [(i, (i + 2 * steps) % 8) for i in range(8)])


def along_x(block):
    return lax.ppermute(block, "fsdp", [(i, i ^ 1) for i in range(8)])


def exchange(blocks, axis, groups=None):
    return lax.all_to_all(blocks, axis, 0, 0, axis_index_groups=groups, tiled=True)


def after(block, other):
    return lax.optimization_barrier((block, other))[0]


def repeated(block, count):
    return jnp.broadcast_to(block[None], (count,) + block.shape)


def dims(matrix, other, left, right):
    return lax.dot_general(
        matrix, other, (((left,), (right,)), ((), ())), preferred_element_type=F32
    )


def dot(matrix, other):
    return dims(matrix, other, 1, 0)


def split_low(value):
    high = value.astype(LOW)
    return high, (value - high.astype(F32)).astype(LOW)


def norm_forward(hidden, gain, shift):
    center = hidden - jnp.mean(hidden, axis=-1, keepdims=True)
    scale = lax.rsqrt(jnp.mean(center * center, axis=-1, keepdims=True) + EPSILON)
    unit = center * scale
    return unit * gain + shift, unit, scale


def norm_backward(grad, unit, scale, gain):
    inner = grad * gain
    mean_inner = jnp.mean(inner, axis=-1, keepdims=True)
    mean_unit = jnp.mean(inner * unit, axis=-1, keepdims=True)
    back = scale * (inner - mean_inner - unit * mean_unit)
    return back, jnp.sum(grad * unit, axis=0), jnp.sum(grad, axis=0)


def pack_kernel(ctx, w_query, w_key, w_value, vectors, heads, turned):
    at = ctx[0]
    for index, ref in enumerate((w_query, w_key, w_value)):
        pair = ref[:, pl.ds(pl.multiple_of((at >> 1) * ROWS, ROWS), ROWS)]
        turned[...] = pair.astype(F32).T
        column = turned[pl.ds(pl.multiple_of((at & 1) * HEAD, HEAD), HEAD), :].astype(LOW)
        for f in range(8):
            heads[f, index * HEAD : (index + 1) * HEAD, :] = column
    for f in range(8):
        heads[f, 3 * HEAD :, :] = vectors[...]


def weights_kernel(ctx, w_out, w_up, w_down, early, late):
    at = ctx[0]
    core = at & 1
    quarter = ((at >> 2) & 1) * 2 + core
    for f in range(8):
        early[f, :64, :] = w_out[pl.ds(pl.multiple_of(core * 64, 64), 64), :]
        late[f] = w_down[pl.ds(pl.multiple_of(quarter * ROWS, ROWS), ROWS), :]
        for block in range(8):
            span = pl.ds(pl.multiple_of(block * 512 + quarter * ROWS, ROWS), ROWS)
            early[f, 64:, block * ROWS : (block + 1) * ROWS] = w_up[:, span]


def forward_kernel(order, *refs):
    parts = refs[:8]
    w_ref, bias_q, bias_v, qkv, rows, mixed_low, mixed, total, held = refs[8:]
    weight = jnp.concatenate([w_ref[f, : 3 * HEAD, :] for f in range(8)], axis=1)
    for index in range(LENGTH // QUERIES):
        span = slice(index * QUERIES, (index + 1) * QUERIES)
        product = dims(weight, parts[index][...], 1, 1)
        query = (product[:HEAD] + bias_q[...]) * (HEAD**-0.5)
        value = product[2 * HEAD :] + bias_v[...]
        pair = jnp.concatenate([product[HEAD : 2 * HEAD], value], axis=0)
        qkv[:HEAD, span] = query.astype(LOW)
        qkv[HEAD:, span] = pair.astype(LOW)
        rows[span, :] = pair.T.astype(LOW)

    def step(index, carry):
        span = pl.ds(pl.multiple_of(index * QUERIES, QUERIES), QUERIES)
        query = qkv[:HEAD, span]
        padded = jnp.concatenate([query, jnp.zeros_like(query)], axis=0)
        peak = None
        for at in range(0, LENGTH, CHUNK):
            scores = dot(rows[at : at + CHUNK, :], padded)
            held[at : at + CHUNK, :] = scores
            top = jnp.max(scores, axis=0, keepdims=True)
            peak = top if peak is None else jnp.maximum(peak, top)
        weight_sum = jnp.zeros((1, QUERIES), F32)
        acc = jnp.zeros((HEAD, QUERIES), F32)
        for at in range(0, LENGTH, CHUNK):
            weights = jnp.exp(held[at : at + CHUNK, :] - peak)
            weight_sum += jnp.sum(weights, axis=0, keepdims=True)
            acc += dot(qkv[2 * HEAD :, at : at + CHUNK], weights.astype(LOW))
        acc = acc / weight_sum
        mixed[:, span] = acc
        total[:, span] = peak + jnp.log(weight_sum)
        mixed_low[order[2 * index]] = acc[:, :ROWS].astype(LOW)
        mixed_low[order[2 * index + 1]] = acc[:, ROWS:].astype(LOW)
        return carry

    lax.fori_loop(0, LENGTH // QUERIES, step, 0)


def backward_kernel(order, grad_ref, qkv, rows, mixed, total, kept, key_acc, value_acc):
    key_acc[...] = jnp.zeros_like(key_acc)
    value_acc[...] = jnp.zeros_like(value_acc)

    def step(index, carry):
        span = pl.ds(pl.multiple_of(index * QUERIES, QUERIES), QUERIES)
        first, second = order[2 * index], order[2 * index + 1]
        query = qkv[:HEAD, span]
        grad = jnp.concatenate([grad_ref[first], grad_ref[second]], axis=1)
        delta = jnp.sum(grad.astype(F32) * mixed[:, span], axis=0, keepdims=True)
        log_total = total[:, span]
        query_pad = jnp.concatenate([query, jnp.zeros_like(query)], axis=0)
        grad_pad = jnp.concatenate([jnp.zeros_like(grad), grad], axis=0)
        query_grad = jnp.zeros((HEAD, QUERIES), F32)
        for at in range(0, LENGTH, CHUNK):
            block = rows[at : at + CHUNK, :]
            chances = jnp.exp(dot(block, query_pad) - log_total)
            chance_grad = dot(block, grad_pad)
            score_grad = (chances * (chance_grad - delta)).astype(LOW)
            value_acc[:, at : at + CHUNK] += dims(grad, chances.astype(LOW), 1, 1)
            key_acc[:, at : at + CHUNK] += dims(query, score_grad, 1, 1)
            query_grad += dot(qkv[HEAD : 2 * HEAD, at : at + CHUNK], score_grad)
        kept[:HEAD, span] = (query_grad * (HEAD**-0.5)).astype(LOW)
        return carry

    lax.fori_loop(0, LENGTH // QUERIES, step, 0)
    kept[HEAD : 2 * HEAD, :] = key_acc[...].astype(LOW)
    kept[2 * HEAD :, :] = value_acc[...].astype(LOW)


def quarter_kernel(down, up, out, sums_ref, message):
    for e in range(4):
        message[e, :32, :] = down[e * 32 : (e + 1) * 32, :].astype(LOW)
        message[e, 32:64, :] = up[e * 32 : (e + 1) * 32, :].astype(LOW)
        rows = [out[f, e * 8 : (e + 1) * 8, :] for f in range(8)]
        message[e, 64:128, :] = jnp.concatenate(rows, axis=0).astype(LOW)
        sums = sums_ref[e]
        high = sums.astype(LOW).astype(F32)
        tail = jnp.concatenate([high, sums - high], axis=0)
        message[e, 128:, :] = tail.astype(LOW)


def input_kernel(grads, w_ref, *outs):
    weight = jnp.concatenate([w_ref[f, : 3 * HEAD, :] for f in range(8)], axis=1)
    for index, out in enumerate(outs):
        span = slice(index * QUERIES, (index + 1) * QUERIES)
        out[...] = dims(grads[:, span], weight, 0, 0).astype(LOW)


def projection_kernel(grads, *refs):
    parts, message = refs[:8], refs[8]
    acc = None
    for index in range(LENGTH // QUERIES):
        span = slice(index * QUERIES, (index + 1) * QUERIES)
        term = dot(grads[:, span], parts[index][...])
        acc = term if acc is None else acc + term
    sums = dims(jnp.ones((8, LENGTH), LOW), grads[...], 1, 1)[:1]
    sums = jnp.concatenate([sums, jnp.zeros((1, HEAD), F32)], axis=1)
    high = sums.astype(LOW).astype(F32)
    tail = jnp.concatenate([high, sums - high, jnp.zeros((1, 512), F32)], axis=1)
    tail = jnp.concatenate([tail, jnp.zeros((7, WIDTH), F32)], axis=0)
    for f in range(8):
        span = slice(f * ROWS, (f + 1) * ROWS)
        wide = jnp.concatenate([acc[j * 24 : (j + 1) * 24, span] for j in range(8)], axis=1)
        message[f] = jnp.concatenate([wide, tail], axis=0).astype(LOW)


def assembly_kernel(ctx, mine, theirs, down, up, out, query, key, value):
    core = ctx[0] & 1
    for side, ref in enumerate((mine, theirs)):
        place = core if side == 0 else 1 - core
        for e in range(8):
            high, low, x = e >> 2, (e >> 1) & 1, e & 1
            part, quarter = high * 2 + x, low * 2 + place
            row = pl.multiple_of(quarter * ROWS + part * 32, 32)
            down[pl.ds(row, 32), :] = ref[e, :32, :].astype(F32)
            block = ref[e, 32:64, :].astype(F32)
            for f in range(8):
                span = pl.ds(pl.multiple_of(f * 512 + quarter * ROWS, ROWS), ROWS)
                up[part * 32 : (part + 1) * 32, span] = block[:, f * ROWS : (f + 1) * ROWS]
            row = pl.multiple_of(place * 64 + low * 32 + part * 8, 8)
            out[pl.ds(row, 8), :] = ref[e, 64:80, :].astype(F32)[:8]
    for e in range(8):
        own = mine[e, 80:112, :].astype(F32)[:24]
        other = theirs[e, 80:112, :].astype(F32)[:24]
        pair = []
        for wide in (jnp.where(core == 0, own, other), jnp.where(core == 0, other, own)):
            pair.append(
                jnp.concatenate([wide[:, j * ROWS : (j + 1) * ROWS] for j in range(8)], axis=0)
            )
        for index, ref in enumerate((query, key, value)):
            rows = slice(index * HEAD, (index + 1) * HEAD)
            both = jnp.concatenate([pair[0][rows], pair[1][rows]], axis=0)
            ref[:, e * ROWS : (e + 1) * ROWS] = both.T


def call(kernel, outs, scratch, flops, moved, *operands):
    in_specs = [pl.BlockSpec(memory_space=pltpu.SMEM if operand.dtype == jnp.int32 else pltpu.VMEM) for operand in operands]
    return pl.pallas_call(
        kernel,
        out_shape=[jax.ShapeDtypeStruct(shape, dtype) for shape, dtype in outs],
        in_specs=in_specs,
        out_specs=[pl.BlockSpec(memory_space=pltpu.VMEM)] * len(outs),
        scratch_shapes=scratch,
        compiler_params=pltpu.CompilerParams(vmem_limit_bytes=VMEM_LIMIT),
        cost_estimate=pl.CostEstimate(flops=flops, bytes_accessed=moved, transcendentals=0),
    )(*operands)


def on_device(
    inputs,
    w_query,
    b_query,
    w_key,
    w_value,
    b_value,
    w_out,
    b_out,
    gain_one,
    shift_one,
    w_up,
    b_up,
    w_down,
    b_down,
    gain_two,
    shift_two,
    cotangent,
):
    ctx, fsdp = lax.axis_index("ctx"), lax.axis_index("fsdp")
    core = ctx & 1

    vectors = jnp.concatenate(
        [
            jnp.stack([b_query, b_value, b_out, gain_one, shift_one, b_down, gain_two, shift_two]),
            b_up.reshape(4, ROWS),
            jnp.zeros((4, ROWS), LOW),
        ]
    )
    at = ctx.reshape(1).astype(jnp.int32)
    (heads,) = call(
        pack_kernel,
        [((8, 208, ROWS), LOW)],
        [pltpu.VMEM((ROWS, ROWS), F32)],
        10**6,
        10**6,
        at,
        w_query,
        w_key,
        w_value,
        vectors,
    )
    own = after(inputs.reshape(ROWS, WIDTH), heads)
    heads = exchange(heads, "fsdp")
    pair = jnp.concatenate([own, swap(own, FAR_X)], axis=0)
    pair = after(pair, heads)
    parts = [pair] + [along_y(pair, k) for k in (1, 2, 3)]
    parts = parts + [swap(part, CORE) for part in parts]
    order = jnp.stack(
        [
            (((ctx >> 2) - k) % 4) * 4 + ((ctx & 3) ^ (2 * j + s))
            for s in range(2)
            for k in range(4)
            for j in range(2)
        ]
    ).astype(jnp.int32)

    early, late = call(
        weights_kernel,
        [((8, 64 + ROWS, WIDTH), LOW), ((8, ROWS, WIDTH), LOW)],
        [],
        10**6,
        10**7,
        at,
        w_out,
        w_up,
        w_down,
    )
    early = exchange(after(early, pair), "fsdp")
    vecs = heads[:, 3 * HEAD :, :].astype(F32)

    def whole(index):
        return vecs[:, index, :].reshape(WIDTH)

    vec_query, vec_value, vec_out, gain_a, shift_a, vec_down, gain_b, shift_b = (
        whole(index) for index in range(8)
    )
    quarter = ((ctx >> 2) & 1) * 2 + core
    vec_up = lax.dynamic_slice(vecs, (0, 8 + quarter, 0), (8, 1, ROWS)).reshape(WIDTH)
    bias_q = lax.dynamic_slice(vec_query, (ctx * HEAD,), (HEAD,)).reshape(HEAD, 1)
    bias_v = lax.dynamic_slice(vec_value, (ctx * HEAD,), (HEAD,)).reshape(HEAD, 1)

    def pick(block, index, axis):
        return lax.dynamic_index_in_dim(block, index, axis, keepdims=False)

    def by_core(mine, theirs, axis):
        first, second = jnp.where(core == 0, mine, theirs), jnp.where(core == 0, theirs, mine)
        return jnp.stack([first, second], axis=axis)

    qkv, rows, mixed_low, mixed, total = call(
        forward_kernel,
        [
            ((3 * HEAD, LENGTH), LOW),
            ((LENGTH, 2 * HEAD), LOW),
            ((16, HEAD, ROWS), LOW),
            ((HEAD, LENGTH), F32),
            ((1, LENGTH), F32),
        ],
        [pltpu.VMEM((LENGTH, QUERIES), F32)],
        10**10,
        10**7,
        order,
        *parts,
        heads,
        bias_q,
        bias_v,
    )
    early, mixed_low = lax.optimization_barrier((early, mixed_low))
    context = exchange(mixed_low, "ctx")
    out_mine = early[:, :64].reshape(512, WIDTH)
    out_theirs = swap(out_mine, CORE)
    mat_up = early[:, 64:].reshape(WIDTH, WIDTH)
    mat_down = exchange(after(late, context), "fsdp").reshape(WIDTH, WIDTH)
    context_mine = pick(context.reshape(8, 2, HEAD, ROWS), core, 1).reshape(512, ROWS)
    context_theirs = pick(context.reshape(8, 2, HEAD, ROWS), 1 - core, 1).reshape(512, ROWS)
    context = context.reshape(WIDTH, ROWS)

    def share(block):
        block = jnp.concatenate([block, swap(block, NEAR_Y)], axis=0)
        return jnp.concatenate([block, swap(block, CORE)], axis=0)

    def collect(partial):
        half = partial[: 2 * ROWS] + swap(partial[2 * ROWS :], CORE)
        return half[:ROWS] + swap(half[ROWS:].astype(LOW), NEAR_Y).astype(F32)

    branch = dims(context_mine, out_mine, 0, 0) + dims(context_theirs, out_theirs, 0, 0) + vec_out
    first, unit_one, scale_one = norm_forward(own.astype(F32) + branch, gain_a, shift_a)
    first_all = share(first.astype(LOW))
    hidden = dot(first_all, mat_up) + vec_up
    gate = 0.5 * (1.0 + lax.erf(hidden * (0.5**0.5)))
    slope = gate + hidden * jnp.exp(-0.5 * hidden * hidden) * 0.3989422804014327
    active = (hidden * gate).astype(LOW)
    second = collect(dot(active, mat_down)) + vec_down
    result, unit_two, scale_two = norm_forward(first + second, gain_b, shift_b)

    grad_out = cotangent.reshape(ROWS, WIDTH).astype(F32)
    grad_two, grad_gain_b, grad_shift_b = norm_backward(grad_out, unit_two, scale_two, gain_b)
    grad_second = grad_two.astype(LOW)
    grad_vec_down = jnp.sum(grad_second.astype(F32), axis=0)
    second_all = share(grad_second)
    down = dims(active, second_all, 0, 0).astype(LOW).reshape(4, 2, ROWS, WIDTH)
    z, low_x, low_y = fsdp >> 1, fsdp & 1, (ctx >> 2) & 1
    down_found = [along_z(pick(down, (z + k) % 4, 0), k) for k in (1, 3, 2)]
    grad_hidden = (slope * dims(second_all, mat_down, 1, 1)).astype(LOW)
    grad_vec_up = jnp.sum(grad_hidden.astype(F32), axis=0)
    grad_first = grad_two + collect(dims(grad_hidden, mat_up, 1, 1))
    grad_one, grad_gain_a, grad_shift_a = norm_backward(grad_first, unit_one, scale_one, gain_a)
    grad_branch = grad_one.astype(LOW)
    grad_vec_out = jnp.sum(grad_branch.astype(F32), axis=0)
    grad_context = by_core(
        dims(out_mine, grad_branch, 1, 1).reshape(8, HEAD, ROWS),
        dims(out_theirs, grad_branch, 1, 1).reshape(8, HEAD, ROWS),
        1,
    )
    grad_context = grad_context.astype(LOW).reshape(16, HEAD, ROWS)
    grad_heads = exchange(grad_context, "ctx")
    out = dot(context, grad_branch).astype(LOW).reshape(8, 2, 2, 32, WIDTH)
    out = pick(out, core, 1).astype(F32) + swap(pick(out, 1 - core, 1), CORE).astype(F32)
    grad_heads = after(grad_heads, out)
    out = pick(out, low_y, 1) + swap(pick(out, 1 - low_y, 1).astype(LOW), NEAR_Y).astype(F32)
    (kept,) = call(
        backward_kernel,
        [((3 * HEAD, LENGTH), LOW)],
        [pltpu.VMEM((HEAD, LENGTH), F32), pltpu.VMEM((HEAD, LENGTH), F32)],
        10**10,
        10**7,
        order,
        grad_heads,
        qkv,
        rows,
        mixed,
        total,
    )
    up = dims(first_all, grad_hidden, 0, 0).astype(LOW).reshape(4, 2, ROWS, WIDTH)
    up_found = along_x(pick(up, 1 - low_x, 1))
    down_found, up_found = after((down_found, up_found), grad_context)
    down = pick(down, z, 0).astype(F32)
    for part in down_found:
        down += part.astype(F32)
    up = pick(up, low_x, 1).astype(F32) + up_found.astype(F32)
    down_found = along_x(pick(down, 1 - low_x, 0).astype(LOW))
    up_found = [along_z(pick(up, (z + k) % 4, 0).astype(LOW), k) for k in (1, 3, 2)]
    down_found, up_found = after((down_found, up_found), grad_heads)
    down = pick(down, low_x, 0) + down_found.astype(F32)
    up = pick(up, z, 0)
    for part in up_found:
        up += part.astype(F32)
    sums = jnp.stack(
        [
            grad_vec_out,
            grad_gain_a,
            grad_shift_a,
            grad_vec_down,
            grad_gain_b,
            grad_shift_b,
            grad_vec_up,
            jnp.zeros_like(grad_vec_up),
        ]
    )
    sums = sums.reshape(8, 4, 2, ROWS).transpose(1, 2, 0, 3).reshape(4, 2, WIDTH)
    sums = jnp.concatenate([sums, jnp.zeros((4, 6, WIDTH), F32)], axis=1)
    (message,) = call(
        quarter_kernel, [((4, 144, WIDTH), LOW)], [], 10**6, 10**7, down, up, out, sums
    )
    kept_later = after(kept, message)
    summed = exchange(message, "ctx", SAME_QUARTER)
    summed = jnp.sum(summed.astype(F32), axis=0)
    hidden_rows = summed[:64]
    sums = jnp.zeros((8, WIDTH), F32)
    piece = (ctx >> 3) * 2 + ((ctx >> 1) & 1)
    sums = lax.dynamic_update_slice(sums, summed[128:130] + summed[136:138], (piece * 2, 0))
    sums = [part.reshape(8, 1, WIDTH) for part in split_low(sums)]
    extra = jnp.concatenate(
        [summed[64:128].reshape(8, 8, WIDTH).astype(LOW), *sums, jnp.zeros((8, 6, WIDTH), LOW)],
        axis=1,
    )

    shares = call(
        input_kernel, [((QUERIES, WIDTH), LOW)] * 8, [], 10**9, 10**7, kept_later, heads
    )
    theirs = [swap(share, CORE) for share in shares[4:]]
    shares = [mine.astype(F32) + other.astype(F32) for mine, other in zip(shares[:4], theirs)]
    pair, sent = shares[0], [share.astype(LOW) for share in shares[1:]]
    for k in (1, 3, 2):
        pair += along_y(sent[k - 1], -k).astype(F32)
    grad_in = grad_one + pair[:ROWS] + swap(pair[ROWS:].astype(LOW), FAR_X).astype(F32)

    (message,) = call(projection_kernel, [((8, 32, WIDTH), LOW)], [], 10**9, 10**7, kept_later, *parts)
    message = jnp.concatenate([message, extra], axis=1)
    summed = jnp.sum(exchange(after(message, sent), "fsdp").astype(F32), axis=0)
    head_sums = summed[24:25, :512]
    head_sums = head_sums[:, :256] + head_sums[:, 256:]
    head_sums = jnp.concatenate([head_sums, jnp.zeros((1, 768), F32)], axis=1)

    def with_sums(blocks, sums):
        rest = jnp.zeros((6, WIDTH), LOW)
        return [blocks.astype(LOW), *split_low(sums), rest]

    message = jnp.concatenate(
        [
            hidden_rows.astype(LOW),
            *with_sums(summed[32:40], summed[40:41] + summed[41:42]),
            *with_sums(summed[:24], head_sums),
        ],
        axis=0,
    )
    message = after(message, pair)
    shared = exchange(repeated(message, 8), "ctx", SAME_CORE)
    shared = after(shared, grad_in)
    shared_theirs = swap(shared, CORE)
    square = ((ROWS, WIDTH), F32)
    grad_mat_down, grad_mat_up, grad_mat_out, grad_mat_query, grad_mat_key, grad_mat_value = call(
        assembly_kernel,
        [((512, WIDTH), F32), ((ROWS, 4096), F32), square, square, square, square],
        [],
        10**6,
        10**7,
        at,
        shared,
        shared_theirs,
    )

    def joined(block):
        return block[0].astype(F32) + block[1].astype(F32)

    holder = (z >> 1) * 4 + (z & 1)
    sums = jnp.stack([joined(pick(shared, holder + e, 0)[72:74]) for e in (0, 2)])
    sums_theirs = jnp.stack([joined(pick(shared_theirs, holder + e, 0)[72:74]) for e in (0, 2)])
    sums = by_core(sums, sums_theirs, 1).reshape(4, 8, ROWS)
    grad_vec_up = sums[:, 6].reshape(512)
    vector_grads = jnp.sum(sums[:, :6], axis=0)
    head_sums = by_core(pick(shared, fsdp, 0)[104:106], pick(shared_theirs, fsdp, 0)[104:106], 0)
    head_sums = (head_sums[:, 0].astype(F32) + head_sums[:, 1].astype(F32)).reshape(2, 8, ROWS)
    grad_vec_query = head_sums[:, 0, :HEAD].reshape(ROWS)
    grad_vec_value = head_sums[:, 1, :HEAD].reshape(ROWS)

    return (
        result.reshape(1, ROWS, WIDTH).astype(LOW),
        grad_in.reshape(1, ROWS, WIDTH),
        grad_mat_query,
        grad_vec_query,
        grad_mat_key,
        grad_mat_value,
        grad_vec_value,
        grad_mat_out,
        vector_grads[0],
        vector_grads[1],
        vector_grads[2],
        grad_mat_up,
        grad_vec_up,
        grad_mat_down,
        vector_grads[3],
        vector_grads[4],
        vector_grads[5],
    )


def solution(mesh):
    tokens, matrix, vector = P("fsdp", "ctx", None), P("fsdp", None), P("fsdp")
    return jax.shard_map(
        on_device,
        mesh=mesh,
        in_specs=(
            tokens,
            matrix,
            vector,
            matrix,
            matrix,
            vector,
            matrix,
            vector,
            vector,
            vector,
            matrix,
            vector,
            matrix,
            vector,
            vector,
            vector,
            tokens,
        ),
        out_specs=(
            tokens,
            tokens,
            matrix,
            vector,
            matrix,
            matrix,
            vector,
            matrix,
            vector,
            vector,
            vector,
            matrix,
            vector,
            matrix,
            vector,
            vector,
            vector,
        ),
        check_vma=False,
    )
```

```python
import functools

import jax
import jax.numpy as jnp
from jax import lax
from jax.experimental import pallas as pl
from jax.experimental.pallas import tpu as pltpu
from jax.sharding import PartitionSpec as P

EPSILON = 1e-05
LOW = jnp.bfloat16
F32 = jnp.float32
WIDTH = 1024
HEAD = 64
ROWS = 128
LENGTH = 2048
CHUNK = 512
QUERIES = 256
SAME_CORE = [list(range(0, 16, 2)), list(range(1, 16, 2))]
SAME_QUARTER = [
    [(high * 2 + low) * 4 + x * 2 + core for high in range(2) for x in range(2)]
    for low in range(2)
    for core in range(2)
]
CORE, FAR_X, NEAR_Y = 1, 2, 4
VMEM_LIMIT = 50 * 1024 * 1024


def swap(block, bit):
    return lax.ppermute(block, "ctx", [(i, i ^ bit) for i in range(16)])


def along_y(block, steps):
    return lax.ppermute(block, "ctx", [(i, (i + 4 * steps) % 16) for i in range(16)])


def along_z(block, steps):
    return lax.ppermute(block, "fsdp", [(i, (i + 2 * steps) % 8) for i in range(8)])


def along_x(block):
    return lax.ppermute(block, "fsdp", [(i, i ^ 1) for i in range(8)])


def exchange(blocks, axis, groups=None):
    return lax.all_to_all(blocks, axis, 0, 0, axis_index_groups=groups, tiled=True)


def after(block, other):
    return lax.optimization_barrier((block, other))[0]


def repeated(block, count):
    return jnp.broadcast_to(block[None], (count,) + block.shape)


def dims(matrix, other, left, right):
    return lax.dot_general(
        matrix, other, (((left,), (right,)), ((), ())), preferred_element_type=F32
    )


def dot(matrix, other):
    return dims(matrix, other, 1, 0)


def split_low(value):
    high = value.astype(LOW)
    return high, (value - high.astype(F32)).astype(LOW)


def norm_forward(hidden, gain, shift):
    center = hidden - jnp.mean(hidden, axis=-1, keepdims=True)
    scale = lax.rsqrt(jnp.mean(center * center, axis=-1, keepdims=True) + EPSILON)
    unit = center * scale
    return unit * gain + shift, unit, scale


def norm_backward(grad, unit, scale, gain):
    inner = grad * gain
    mean_inner = jnp.mean(inner, axis=-1, keepdims=True)
    mean_unit = jnp.mean(inner * unit, axis=-1, keepdims=True)
    back = scale * (inner - mean_inner - unit * mean_unit)
    return back, jnp.sum(grad * unit, axis=0), jnp.sum(grad, axis=0)


def pack_kernel(ctx, w_query, w_key, w_value, vectors, heads, turned):
    at = ctx[0]
    for index, ref in enumerate((w_query, w_key, w_value)):
        pair = ref[:, pl.ds(pl.multiple_of((at >> 1) * ROWS, ROWS), ROWS)]
        turned[...] = pair.astype(F32).T
        column = turned[pl.ds(pl.multiple_of((at & 1) * HEAD, HEAD), HEAD), :].astype(LOW)
        for f in range(8):
            heads[f, index * HEAD : (index + 1) * HEAD, :] = column
    for f in range(8):
        heads[f, 3 * HEAD :, :] = vectors[...]


def weights_kernel(ctx, w_out, w_up, w_down, early, late):
    at = ctx[0]
    core = at & 1
    quarter = ((at >> 2) & 1) * 2 + core
    for f in range(8):
        early[f, :64, :] = w_out[pl.ds(pl.multiple_of(core * 64, 64), 64), :]
        late[f] = w_down[pl.ds(pl.multiple_of(quarter * ROWS, ROWS), ROWS), :]
        for block in range(8):
            span = pl.ds(pl.multiple_of(block * 512 + quarter * ROWS, ROWS), ROWS)
            early[f, 64:, block * ROWS : (block + 1) * ROWS] = w_up[:, span]


def forward_kernel(order, *refs):
    parts = refs[:8]
    w_ref, bias_q, bias_v, qkv, rows, mixed_low, mixed, total, own_weight, held = refs[8:]
    weight = jnp.concatenate([w_ref[f, : 3 * HEAD, :] for f in range(8)], axis=1)
    own_weight[...] = weight
    for index in range(LENGTH // QUERIES):
        span = slice(index * QUERIES, (index + 1) * QUERIES)
        product = dims(weight, parts[index][...], 1, 1)
        query = (product[:HEAD] + bias_q[...]) * (HEAD**-0.5)
        value = product[2 * HEAD :] + bias_v[...]
        pair = jnp.concatenate([product[HEAD : 2 * HEAD], value], axis=0)
        qkv[:HEAD, span] = query.astype(LOW)
        qkv[HEAD:, span] = pair.astype(LOW)
        rows[span, :] = pair.T.astype(LOW)

    def step(index, carry):
        span = pl.ds(pl.multiple_of(index * QUERIES, QUERIES), QUERIES)
        query = qkv[:HEAD, span]
        padded = jnp.concatenate([query, jnp.zeros_like(query)], axis=0)
        peak = None
        for at in range(0, LENGTH, CHUNK):
            scores = dot(rows[at : at + CHUNK, :], padded)
            held[at : at + CHUNK, :] = scores
            top = jnp.max(scores, axis=0, keepdims=True)
            peak = top if peak is None else jnp.maximum(peak, top)
        weight_sum = jnp.zeros((1, QUERIES), F32)
        acc = jnp.zeros((HEAD, QUERIES), F32)
        for at in range(0, LENGTH, CHUNK):
            weights = jnp.exp(held[at : at + CHUNK, :] - peak)
            weight_sum += jnp.sum(weights, axis=0, keepdims=True)
            acc += dot(qkv[2 * HEAD :, at : at + CHUNK], weights.astype(LOW))
        acc = acc / weight_sum
        mixed[:, span] = acc
        total[:, span] = peak + jnp.log(weight_sum)
        mixed_low[order[2 * index]] = acc[:, :ROWS].astype(LOW)
        mixed_low[order[2 * index + 1]] = acc[:, ROWS:].astype(LOW)
        return carry

    lax.fori_loop(0, LENGTH // QUERIES, step, 0)


def backward_kernel(order, grad_ref, qkv, rows, mixed, total, *refs):
    parts, weight = refs[:8], refs[8]
    message, shares = refs[9], refs[10:18]
    kept, key_acc, value_acc = refs[18:]
    key_acc[...] = jnp.zeros_like(key_acc)
    value_acc[...] = jnp.zeros_like(value_acc)

    def step(index, carry):
        span = pl.ds(pl.multiple_of(index * QUERIES, QUERIES), QUERIES)
        first, second = order[2 * index], order[2 * index + 1]
        query = qkv[:HEAD, span]
        grad = jnp.concatenate([grad_ref[first], grad_ref[second]], axis=1)
        delta = jnp.sum(grad.astype(F32) * mixed[:, span], axis=0, keepdims=True)
        log_total = total[:, span]
        query_pad = jnp.concatenate([query, jnp.zeros_like(query)], axis=0)
        grad_pad = jnp.concatenate([jnp.zeros_like(grad), grad], axis=0)
        query_grad = jnp.zeros((HEAD, QUERIES), F32)
        for at in range(0, LENGTH, CHUNK):
            block = rows[at : at + CHUNK, :]
            chances = jnp.exp(dot(block, query_pad) - log_total)
            chance_grad = dot(block, grad_pad)
            score_grad = (chances * (chance_grad - delta)).astype(LOW)
            value_acc[:, at : at + CHUNK] += dims(grad, chances.astype(LOW), 1, 1)
            key_acc[:, at : at + CHUNK] += dims(query, score_grad, 1, 1)
            query_grad += dot(qkv[HEAD : 2 * HEAD, at : at + CHUNK], score_grad)
        kept[:HEAD, span] = (query_grad * (HEAD**-0.5)).astype(LOW)
        return carry

    lax.fori_loop(0, LENGTH // QUERIES, step, 0)
    kept[HEAD : 2 * HEAD, :] = key_acc[...].astype(LOW)
    kept[2 * HEAD :, :] = value_acc[...].astype(LOW)
    acc = None
    for index in range(LENGTH // QUERIES):
        span = slice(index * QUERIES, (index + 1) * QUERIES)
        term = dot(kept[:, span], parts[index][...])
        acc = term if acc is None else acc + term
    sums = dims(jnp.ones((8, LENGTH), LOW), kept[...], 1, 1)[:1]
    sums = jnp.concatenate([sums, jnp.zeros((1, HEAD), F32)], axis=1)
    high = sums.astype(LOW).astype(F32)
    tail = jnp.concatenate([high, sums - high, jnp.zeros((1, 512), F32)], axis=1)
    tail = jnp.concatenate([tail, jnp.zeros((7, WIDTH), F32)], axis=0)
    for f in range(8):
        span = slice(f * ROWS, (f + 1) * ROWS)
        wide = jnp.concatenate([acc[j * 24 : (j + 1) * 24, span] for j in range(8)], axis=1)
        message[f] = jnp.concatenate([wide, tail], axis=0).astype(LOW)
    for index, share in enumerate(shares):
        span = slice(index * QUERIES, (index + 1) * QUERIES)
        share[...] = dims(kept[:, span], weight[...], 0, 0).astype(LOW)


def quarter_kernel(out, sums_ref, message):
    for e in range(4):
        rows = [out[f, e * 16 : (e + 1) * 16, :] for f in range(8)]
        message[e, :128, :] = jnp.concatenate(rows, axis=0).astype(LOW)
        sums = sums_ref[e]
        high = sums.astype(LOW).astype(F32)
        tail = jnp.concatenate([high, sums - high], axis=0)
        message[e, 128:, :] = tail.astype(LOW)


def extra_kernel(ctx, found, heads, message):
    piece = (ctx[0] >> 3) * 2 + ((ctx[0] >> 1) & 1)
    total = found[0].astype(F32)
    for index in range(1, 4):
        total += found[index].astype(F32)
    sums = total[128:136] + total[136:144]
    for f in range(8):
        row = jnp.where(f >> 1 == piece, sums[f & 1 : (f & 1) + 1], 0.0)
        high = row.astype(LOW).astype(F32)
        tail = jnp.concatenate([high, row - high, jnp.zeros((14, WIDTH), F32)], axis=0)
        message[f, :32, :] = heads[f]
        message[f, 32:48, :] = total[f * 16 : (f + 1) * 16].astype(LOW)
        message[f, 48:, :] = tail.astype(LOW)


def assembly_kernel(ctx, mine, theirs, down, up, out, query, key, value):
    core = ctx[0] & 1
    for side, ref in enumerate((mine, theirs)):
        place = core if side == 0 else 1 - core
        for e in range(8):
            high, low, x = e >> 2, (e >> 1) & 1, e & 1
            part, quarter = high * 2 + x, low * 2 + place
            row = pl.multiple_of(quarter * ROWS + part * 32, 32)
            down[pl.ds(row, 32), :] = ref[e, :32, :].astype(F32)
            block = ref[e, 32:64, :].astype(F32)
            for f in range(8):
                span = pl.ds(pl.multiple_of(f * 512 + quarter * ROWS, ROWS), ROWS)
                up[part * 32 : (part + 1) * 32, span] = block[:, f * ROWS : (f + 1) * ROWS]
            if low == 0:
                row = pl.multiple_of(place * 64 + part * 16, 16)
                pair = ref[e, 64:80, :].astype(F32) + ref[e + 2, 64:80, :].astype(F32)
                out[pl.ds(row, 16), :] = pair
    for e in range(8):
        own = mine[e, 80:112, :].astype(F32)[:24]
        other = theirs[e, 80:112, :].astype(F32)[:24]
        pair = []
        for wide in (jnp.where(core == 0, own, other), jnp.where(core == 0, other, own)):
            pair.append(
                jnp.concatenate([wide[:, j * ROWS : (j + 1) * ROWS] for j in range(8)], axis=0)
            )
        for index, ref in enumerate((query, key, value)):
            rows = slice(index * HEAD, (index + 1) * HEAD)
            both = jnp.concatenate([pair[0][rows], pair[1][rows]], axis=0)
            ref[:, e * ROWS : (e + 1) * ROWS] = both.T


def call(kernel, outs, scratch, flops, moved, *operands):
    in_specs = [pl.BlockSpec(memory_space=pltpu.SMEM if operand.dtype == jnp.int32 else pltpu.VMEM) for operand in operands]
    return pl.pallas_call(
        kernel,
        out_shape=[jax.ShapeDtypeStruct(shape, dtype) for shape, dtype in outs],
        in_specs=in_specs,
        out_specs=[pl.BlockSpec(memory_space=pltpu.VMEM)] * len(outs),
        scratch_shapes=scratch,
        compiler_params=pltpu.CompilerParams(vmem_limit_bytes=VMEM_LIMIT),
        cost_estimate=pl.CostEstimate(flops=flops, bytes_accessed=moved, transcendentals=0),
    )(*operands)


def on_device(
    inputs,
    w_query,
    b_query,
    w_key,
    w_value,
    b_value,
    w_out,
    b_out,
    gain_one,
    shift_one,
    w_up,
    b_up,
    w_down,
    b_down,
    gain_two,
    shift_two,
    cotangent,
):
    ctx, fsdp = lax.axis_index("ctx"), lax.axis_index("fsdp")
    core = ctx & 1

    vectors = jnp.concatenate(
        [
            jnp.stack([b_query, b_value, b_out, gain_one, shift_one, b_down, gain_two, shift_two]),
            b_up.reshape(4, ROWS),
            jnp.zeros((4, ROWS), LOW),
        ]
    )
    at = ctx.reshape(1).astype(jnp.int32)
    (heads,) = call(
        pack_kernel,
        [((8, 208, ROWS), LOW)],
        [pltpu.VMEM((ROWS, ROWS), F32)],
        10**6,
        10**6,
        at,
        w_query,
        w_key,
        w_value,
        vectors,
    )
    own = after(inputs.reshape(ROWS, WIDTH), heads)
    heads = exchange(heads, "fsdp")
    pair = jnp.concatenate([own, swap(own, FAR_X)], axis=0)
    pair = after(pair, heads)
    parts = [pair] + [along_y(pair, k) for k in (1, 2, 3)]
    parts = parts + [swap(part, CORE) for part in parts]
    order = jnp.stack(
        [
            (((ctx >> 2) - k) % 4) * 4 + ((ctx & 3) ^ (2 * j + s))
            for s in range(2)
            for k in range(4)
            for j in range(2)
        ]
    ).astype(jnp.int32)

    early, late = call(
        weights_kernel,
        [((8, 64 + ROWS, WIDTH), LOW), ((8, ROWS, WIDTH), LOW)],
        [],
        10**6,
        10**7,
        at,
        w_out,
        w_up,
        w_down,
    )
    early = exchange(after(early, pair), "fsdp")
    vecs = heads[:, 3 * HEAD :, :].astype(F32)

    def whole(index):
        return vecs[:, index, :].reshape(WIDTH)

    vec_query, vec_value, vec_out, gain_a, shift_a, vec_down, gain_b, shift_b = (
        whole(index) for index in range(8)
    )
    quarter = ((ctx >> 2) & 1) * 2 + core
    vec_up = lax.dynamic_slice(vecs, (0, 8 + quarter, 0), (8, 1, ROWS)).reshape(WIDTH)
    bias_q = lax.dynamic_slice(vec_query, (ctx * HEAD,), (HEAD,)).reshape(HEAD, 1)
    bias_v = lax.dynamic_slice(vec_value, (ctx * HEAD,), (HEAD,)).reshape(HEAD, 1)

    def pick(block, index, axis):
        return lax.dynamic_index_in_dim(block, index, axis, keepdims=False)

    def by_core(mine, theirs, axis):
        first, second = jnp.where(core == 0, mine, theirs), jnp.where(core == 0, theirs, mine)
        return jnp.stack([first, second], axis=axis)

    qkv, rows, mixed_low, mixed, total, own_weight = call(
        forward_kernel,
        [
            ((3 * HEAD, LENGTH), LOW),
            ((LENGTH, 2 * HEAD), LOW),
            ((16, HEAD, ROWS), LOW),
            ((HEAD, LENGTH), F32),
            ((1, LENGTH), F32),
            ((3 * HEAD, WIDTH), LOW),
        ],
        [pltpu.VMEM((LENGTH, QUERIES), F32)],
        10**10,
        10**7,
        order,
        *parts,
        heads,
        bias_q,
        bias_v,
    )
    early, mixed_low = lax.optimization_barrier((early, mixed_low))
    context = exchange(mixed_low, "ctx")
    out_mine = early[:, :64].reshape(512, WIDTH)
    out_theirs = swap(out_mine, CORE)
    mat_up = early[:, 64:].reshape(WIDTH, WIDTH)
    mat_down = exchange(after(late, context), "fsdp").reshape(WIDTH, WIDTH)
    context_mine = pick(context.reshape(8, 2, HEAD, ROWS), core, 1).reshape(512, ROWS)
    context_theirs = pick(context.reshape(8, 2, HEAD, ROWS), 1 - core, 1).reshape(512, ROWS)
    context = context.reshape(WIDTH, ROWS)

    def share(block):
        block = jnp.concatenate([block, swap(block, NEAR_Y)], axis=0)
        return jnp.concatenate([block, swap(block, CORE)], axis=0)

    def collect(partial):
        half = partial[: 2 * ROWS] + swap(partial[2 * ROWS :].astype(LOW), CORE).astype(F32)
        return half[:ROWS] + swap(half[ROWS:].astype(LOW), NEAR_Y).astype(F32)

    branch = dims(context_mine, out_mine, 0, 0) + dims(context_theirs, out_theirs, 0, 0) + vec_out
    first, unit_one, scale_one = norm_forward(own.astype(F32) + branch, gain_a, shift_a)
    first_all = share(first.astype(LOW))
    hidden = dot(first_all, mat_up) + vec_up
    gate = 0.5 * (1.0 + lax.erf(hidden * (0.5**0.5)))
    slope = gate + hidden * jnp.exp(-0.5 * hidden * hidden) * 0.3989422804014327
    active = (hidden * gate).astype(LOW)
    second = collect(dot(active, mat_down)) + vec_down
    result, unit_two, scale_two = norm_forward(first + second, gain_b, shift_b)

    grad_out = cotangent.reshape(ROWS, WIDTH).astype(F32)
    grad_two, grad_gain_b, grad_shift_b = norm_backward(grad_out, unit_two, scale_two, gain_b)
    grad_second = grad_two.astype(LOW)
    grad_vec_down = jnp.sum(grad_second.astype(F32), axis=0)
    second_all = share(grad_second)
    down = dims(active, second_all, 0, 0).astype(LOW).reshape(4, 2, ROWS, WIDTH)
    z, low_x, low_y = fsdp >> 1, fsdp & 1, (ctx >> 2) & 1
    down_found = [along_z(pick(down, (z + k) % 4, 0), k) for k in (1, 3, 2)]
    grad_hidden = (slope * dims(second_all, mat_down, 1, 1)).astype(LOW)
    grad_vec_up = jnp.sum(grad_hidden.astype(F32), axis=0)
    up = dims(first_all, grad_hidden, 0, 0).astype(LOW).reshape(4, 2, ROWS, WIDTH)
    grad_first = grad_two + collect(dims(grad_hidden, mat_up, 1, 1))
    grad_first = after(grad_first, (up, down_found[:2]))
    grad_one, grad_gain_a, grad_shift_a = norm_backward(grad_first, unit_one, scale_one, gain_a)
    grad_branch = grad_one.astype(LOW)
    grad_vec_out = jnp.sum(grad_branch.astype(F32), axis=0)
    grad_context = by_core(
        dims(out_mine, grad_branch, 1, 1).reshape(8, HEAD, ROWS),
        dims(out_theirs, grad_branch, 1, 1).reshape(8, HEAD, ROWS),
        1,
    )
    grad_context = grad_context.astype(LOW).reshape(16, HEAD, ROWS)
    grad_heads = exchange(grad_context, "ctx")
    out = dot(after(context, grad_context), grad_branch).astype(LOW).reshape(8, 2, 64, WIDTH)
    out = pick(out, core, 1).astype(F32) + swap(pick(out, 1 - core, 1), CORE).astype(F32)
    sums = jnp.stack(
        [
            grad_vec_out,
            grad_gain_a,
            grad_shift_a,
            grad_vec_down,
            grad_gain_b,
            grad_shift_b,
            grad_vec_up,
            jnp.zeros_like(grad_vec_up),
        ]
    )
    sums = sums.reshape(8, 4, 2, ROWS).transpose(1, 2, 0, 3).reshape(4, 2, WIDTH)
    sums = jnp.concatenate([sums, jnp.zeros((4, 6, WIDTH), F32)], axis=1)
    (quarter_message,) = call(
        quarter_kernel, [((4, 144, WIDTH), LOW)], [], 10**6, 10**6, out, sums
    )
    summed = exchange(after(quarter_message, grad_heads), "ctx", SAME_QUARTER)
    grad_heads = after(grad_heads, quarter_message)
    message, *shares = call(
        backward_kernel,
        [((8, 32, WIDTH), LOW)] + [((QUERIES, WIDTH), LOW)] * 8,
        [pltpu.VMEM((3 * HEAD, LENGTH), LOW), pltpu.VMEM((HEAD, LENGTH), F32), pltpu.VMEM((HEAD, LENGTH), F32)],
        10**6,
        10**5,
        order,
        grad_heads,
        qkv,
        rows,
        mixed,
        total,
        *parts,
        own_weight,
    )
    up_found = [along_z(pick(up, (z + k) % 4, 0), k) for k in (1, 3, 2)]
    down_found = after([*down_found[:2], after(down_found[2], grad_context)], message)
    theirs = [swap(share, CORE) for share in shares[4:]]
    message = after(message, up_found)
    (message,) = call(
        extra_kernel, [((8, 64, WIDTH), LOW)], [], 10**6, 10**6, at, summed, message
    )
    shares, theirs = after((shares, theirs), message)
    def own_sum(blocks, found):
        total = pick(blocks, z, 0).astype(F32)
        for part in found:
            total += part.astype(F32)
        return pick(total, low_x, 0), along_x(pick(total, 1 - low_x, 0).astype(LOW))

    down, down_found = own_sum(down, down_found)
    down += after(down_found, message).astype(F32)
    up, up_found = own_sum(up, after(up_found, message))
    up += up_found.astype(F32)

    summed = jnp.sum(exchange(message, "fsdp").astype(F32), axis=0)

    shares = [mine.astype(F32) + other.astype(F32) for mine, other in zip(shares[:4], theirs)]
    pair, sent = shares[0], [share.astype(LOW) for share in shares[1:]]
    found = [along_y(sent[k - 1], -k) for k in (1, 3, 2)]

    hidden_rows = jnp.concatenate(
        [down.reshape(4, 32, WIDTH).astype(LOW), up.reshape(4, 32, WIDTH).astype(LOW)], axis=1
    )
    hidden_rows = after(hidden_rows, summed)
    found = after(found, hidden_rows)
    for part in found:
        pair += part.astype(F32)
    grad_in = grad_one + pair[:ROWS] + swap(pair[ROWS:].astype(LOW), FAR_X).astype(F32)
    hidden_rows = exchange(hidden_rows, "ctx", SAME_QUARTER)
    hidden_rows = jnp.sum(hidden_rows.astype(F32), axis=0)
    head_sums = summed[24:25, :512]
    head_sums = head_sums[:, :256] + head_sums[:, 256:]
    head_sums = jnp.concatenate([head_sums, jnp.zeros((1, 768), F32)], axis=1)

    message = jnp.concatenate(
        [
            hidden_rows.astype(LOW),
            summed[32:48].astype(LOW),
            summed[:24].astype(LOW),
            *split_low(head_sums),
            *split_low(summed[48:49] + summed[49:50]),
            jnp.zeros((4, WIDTH), LOW),
        ],
        axis=0,
    )
    message = after(message, pair)
    shared = exchange(repeated(message, 8), "ctx", SAME_CORE)
    shared = after(shared, grad_in)
    shared_theirs = swap(shared, CORE)
    square = ((ROWS, WIDTH), F32)
    grad_mat_down, grad_mat_up, grad_mat_out, grad_mat_query, grad_mat_key, grad_mat_value = call(
        assembly_kernel,
        [((512, WIDTH), F32), ((ROWS, 4096), F32), square, square, square, square],
        [],
        10**6,
        10**7,
        at,
        shared,
        shared_theirs,
    )

    def joined(block):
        return block[0].astype(F32) + block[1].astype(F32)

    holder = (z >> 1) * 4 + (z & 1)
    sums = jnp.stack([joined(pick(shared, holder + e, 0)[106:108]) for e in (0, 2)])
    sums_theirs = jnp.stack([joined(pick(shared_theirs, holder + e, 0)[106:108]) for e in (0, 2)])
    sums = by_core(sums, sums_theirs, 1).reshape(4, 8, ROWS)
    grad_vec_up = sums[:, 6].reshape(512)
    vector_grads = jnp.sum(sums[:, :6], axis=0)
    head_sums = by_core(pick(shared, fsdp, 0)[104:106], pick(shared_theirs, fsdp, 0)[104:106], 0)
    head_sums = (head_sums[:, 0].astype(F32) + head_sums[:, 1].astype(F32)).reshape(2, 8, ROWS)
    grad_vec_query = head_sums[:, 0, :HEAD].reshape(ROWS)
    grad_vec_value = head_sums[:, 1, :HEAD].reshape(ROWS)

    return (
        result.reshape(1, ROWS, WIDTH).astype(LOW),
        grad_in.reshape(1, ROWS, WIDTH),
        grad_mat_query,
        grad_vec_query,
        grad_mat_key,
        grad_mat_value,
        grad_vec_value,
        grad_mat_out,
        vector_grads[0],
        vector_grads[1],
        vector_grads[2],
        grad_mat_up,
        grad_vec_up,
        grad_mat_down,
        vector_grads[3],
        vector_grads[4],
        vector_grads[5],
    )


def solution(mesh):
    tokens, matrix, vector = P("fsdp", "ctx", None), P("fsdp", None), P("fsdp")
    return jax.shard_map(
        on_device,
        mesh=mesh,
        in_specs=(
            tokens,
            matrix,
            vector,
            matrix,
            matrix,
            vector,
            matrix,
            vector,
            vector,
            vector,
            matrix,
            vector,
            matrix,
            vector,
            vector,
            vector,
            tokens,
        ),
        out_specs=(
            tokens,
            tokens,
            matrix,
            vector,
            matrix,
            matrix,
            vector,
            matrix,
            vector,
            vector,
            vector,
            matrix,
            vector,
            matrix,
            vector,
            vector,
            vector,
        ),
        check_vma=False,
    )
```

```python
import functools

import jax
import jax.numpy as jnp
from jax import lax
from jax.experimental import pallas as pl
from jax.experimental.pallas import tpu as pltpu
from jax.sharding import PartitionSpec as P

EPSILON = 1e-05
LOW = jnp.bfloat16
F32 = jnp.float32
WIDTH = 1024
HEAD = 64
ROWS = 128
LENGTH = 2048
CHUNK = 512
QUERIES = 256
SAME_CORE = [list(range(0, 16, 2)), list(range(1, 16, 2))]
SAME_QUARTER = [
    [(high * 2 + low) * 4 + x * 2 + core for high in range(2) for x in range(2)]
    for low in range(2)
    for core in range(2)
]
CORE, FAR_X, NEAR_Y = 1, 2, 4
VMEM_LIMIT = 50 * 1024 * 1024


def swap(block, bit):
    return lax.ppermute(block, "ctx", [(i, i ^ bit) for i in range(16)])


def along_y(block, steps):
    return lax.ppermute(block, "ctx", [(i, (i + 4 * steps) % 16) for i in range(16)])


def along_z(block, steps):
    return lax.ppermute(block, "fsdp", [(i, (i + 2 * steps) % 8) for i in range(8)])


def along_x(block):
    return lax.ppermute(block, "fsdp", [(i, i ^ 1) for i in range(8)])


def exchange(blocks, axis, groups=None):
    return lax.all_to_all(blocks, axis, 0, 0, axis_index_groups=groups, tiled=True)


def after(block, other):
    return lax.optimization_barrier((block, other))[0]


def repeated(block, count):
    return jnp.broadcast_to(block[None], (count,) + block.shape)


def dims(matrix, other, left, right):
    return lax.dot_general(
        matrix, other, (((left,), (right,)), ((), ())), preferred_element_type=F32
    )


def dot(matrix, other):
    return dims(matrix, other, 1, 0)


def split_low(value):
    high = value.astype(LOW)
    return high, (value - high.astype(F32)).astype(LOW)


def norm_forward(hidden, gain, shift):
    center = hidden - jnp.mean(hidden, axis=-1, keepdims=True)
    scale = lax.rsqrt(jnp.mean(center * center, axis=-1, keepdims=True) + EPSILON)
    unit = center * scale
    return unit * gain + shift, unit, scale


def norm_backward(grad, unit, scale, gain):
    inner = grad * gain
    mean_inner = jnp.mean(inner, axis=-1, keepdims=True)
    mean_unit = jnp.mean(inner * unit, axis=-1, keepdims=True)
    back = scale * (inner - mean_inner - unit * mean_unit)
    return back, jnp.sum(grad * unit, axis=0), jnp.sum(grad, axis=0)


def pack_kernel(ctx, w_query, w_key, w_value, vectors, heads, turned):
    at = ctx[0]
    for index, ref in enumerate((w_query, w_key, w_value)):
        pair = ref[:, pl.ds(pl.multiple_of((at >> 1) * ROWS, ROWS), ROWS)]
        turned[...] = pair.astype(F32).T
        column = turned[pl.ds(pl.multiple_of((at & 1) * HEAD, HEAD), HEAD), :].astype(LOW)
        for f in range(8):
            heads[f, index * HEAD : (index + 1) * HEAD, :] = column
    for f in range(8):
        heads[f, 3 * HEAD :, :] = vectors[...]


def weights_kernel(ctx, w_out, w_up, w_down, early, late):
    at = ctx[0]
    core = at & 1
    quarter = ((at >> 2) & 1) * 2 + core
    for f in range(8):
        rows = pl.multiple_of(quarter * ROWS, ROWS)
        early[f, 64 + ROWS :, :] = w_down[pl.ds(rows, 48), :]
        late[f] = w_down[pl.ds(pl.multiple_of(rows + 48, 16), 80), :]
        early[f, :64, :] = w_out[pl.ds(pl.multiple_of(core * 64, 64), 64), :]
        for block in range(8):
            span = pl.ds(pl.multiple_of(block * 512 + quarter * ROWS, ROWS), ROWS)
            early[f, 64 : 64 + ROWS, block * ROWS : (block + 1) * ROWS] = w_up[:, span]


def forward_kernel(order, *refs):
    parts = refs[:8]
    w_ref, bias_q, bias_v, qkv, rows, mixed_low, mixed, total, own_weight, held = refs[8:]
    weight = jnp.concatenate([w_ref[f, : 3 * HEAD, :] for f in range(8)], axis=1)
    own_weight[...] = weight
    for index in range(LENGTH // QUERIES):
        span = slice(index * QUERIES, (index + 1) * QUERIES)
        product = dims(weight, parts[index][...], 1, 1)
        query = (product[:HEAD] + bias_q[...]) * (HEAD**-0.5)
        value = product[2 * HEAD :] + bias_v[...]
        pair = jnp.concatenate([product[HEAD : 2 * HEAD], value], axis=0)
        qkv[:HEAD, span] = query.astype(LOW)
        qkv[HEAD:, span] = pair.astype(LOW)
        rows[span, :] = pair.T.astype(LOW)

    def step(index, carry):
        span = pl.ds(pl.multiple_of(index * QUERIES, QUERIES), QUERIES)
        query = qkv[:HEAD, span]
        padded = jnp.concatenate([query, jnp.zeros_like(query)], axis=0)
        peak = None
        for at in range(0, LENGTH, CHUNK):
            scores = dot(rows[at : at + CHUNK, :], padded)
            held[at : at + CHUNK, :] = scores
            top = jnp.max(scores, axis=0, keepdims=True)
            peak = top if peak is None else jnp.maximum(peak, top)
        weight_sum = jnp.zeros((1, QUERIES), F32)
        acc = jnp.zeros((HEAD, QUERIES), F32)
        for at in range(0, LENGTH, CHUNK):
            weights = jnp.exp(held[at : at + CHUNK, :] - peak)
            weight_sum += jnp.sum(weights, axis=0, keepdims=True)
            acc += dot(qkv[2 * HEAD :, at : at + CHUNK], weights.astype(LOW))
        acc = acc / weight_sum
        mixed[:, span] = acc
        total[:, span] = peak + jnp.log(weight_sum)
        mixed_low[order[2 * index]] = acc[:, :ROWS].astype(LOW)
        mixed_low[order[2 * index + 1]] = acc[:, ROWS:].astype(LOW)
        return carry

    lax.fori_loop(0, LENGTH // QUERIES, step, 0)


def backward_kernel(order, grad_ref, qkv, rows, mixed, total, *refs):
    parts, weight = refs[:8], refs[8]
    message, shares = refs[9], refs[10:18]
    kept, key_acc, value_acc = refs[18:]
    key_acc[...] = jnp.zeros_like(key_acc)
    value_acc[...] = jnp.zeros_like(value_acc)

    def step(index, carry):
        span = pl.ds(pl.multiple_of(index * QUERIES, QUERIES), QUERIES)
        first, second = order[2 * index], order[2 * index + 1]
        query = qkv[:HEAD, span]
        grad = jnp.concatenate([grad_ref[first], grad_ref[second]], axis=1)
        delta = jnp.sum(grad.astype(F32) * mixed[:, span], axis=0, keepdims=True)
        log_total = total[:, span]
        query_pad = jnp.concatenate([query, jnp.zeros_like(query)], axis=0)
        grad_pad = jnp.concatenate([jnp.zeros_like(grad), grad], axis=0)
        query_grad = jnp.zeros((HEAD, QUERIES), F32)
        for at in range(0, LENGTH, CHUNK):
            block = rows[at : at + CHUNK, :]
            chances = jnp.exp(dot(block, query_pad) - log_total)
            chance_grad = dot(block, grad_pad)
            score_grad = (chances * (chance_grad - delta)).astype(LOW)
            value_acc[:, at : at + CHUNK] += dims(grad, chances.astype(LOW), 1, 1)
            key_acc[:, at : at + CHUNK] += dims(query, score_grad, 1, 1)
            query_grad += dot(qkv[HEAD : 2 * HEAD, at : at + CHUNK], score_grad)
        kept[:HEAD, span] = (query_grad * (HEAD**-0.5)).astype(LOW)
        return carry

    lax.fori_loop(0, LENGTH // QUERIES, step, 0)
    kept[HEAD : 2 * HEAD, :] = key_acc[...].astype(LOW)
    kept[2 * HEAD :, :] = value_acc[...].astype(LOW)
    acc = None
    for index in range(LENGTH // QUERIES):
        span = slice(index * QUERIES, (index + 1) * QUERIES)
        term = dot(kept[:, span], parts[index][...])
        acc = term if acc is None else acc + term
    sums = dims(jnp.ones((8, LENGTH), LOW), kept[...], 1, 1)[:1]
    sums = jnp.concatenate([sums, jnp.zeros((1, HEAD), F32)], axis=1)
    high = sums.astype(LOW).astype(F32)
    tail = jnp.concatenate([high, sums - high, jnp.zeros((1, 512), F32)], axis=1)
    tail = jnp.concatenate([tail, jnp.zeros((7, WIDTH), F32)], axis=0)
    for f in range(8):
        span = slice(f * ROWS, (f + 1) * ROWS)
        wide = jnp.concatenate([acc[j * 24 : (j + 1) * 24, span] for j in range(8)], axis=1)
        message[f] = jnp.concatenate([wide, tail], axis=0).astype(LOW)
    for index, share in enumerate(shares):
        span = slice(index * QUERIES, (index + 1) * QUERIES)
        share[...] = dims(kept[:, span], weight[...], 0, 0).astype(LOW)


def quarter_kernel(out, sums_ref, message):
    for e in range(4):
        rows = [out[f, e * 16 : (e + 1) * 16, :] for f in range(8)]
        message[e, :128, :] = jnp.concatenate(rows, axis=0).astype(LOW)
        sums = sums_ref[e]
        high = sums.astype(LOW).astype(F32)
        tail = jnp.concatenate([high, sums - high], axis=0)
        message[e, 128:, :] = tail.astype(LOW)


def extra_kernel(ctx, found, heads, message):
    piece = (ctx[0] >> 3) * 2 + ((ctx[0] >> 1) & 1)
    total = found[0].astype(F32)
    for index in range(1, 4):
        total += found[index].astype(F32)
    sums = total[128:136] + total[136:144]
    for f in range(8):
        row = jnp.where(f >> 1 == piece, sums[f & 1 : (f & 1) + 1], 0.0)
        high = row.astype(LOW).astype(F32)
        tail = jnp.concatenate([high, row - high, jnp.zeros((14, WIDTH), F32)], axis=0)
        message[f, :32, :] = heads[f]
        message[f, 32:48, :] = total[f * 16 : (f + 1) * 16].astype(LOW)
        message[f, 48:, :] = tail.astype(LOW)


def assembly_kernel(ctx, mine, theirs, down, up, out, query, key, value):
    core = ctx[0] & 1
    for side, ref in enumerate((mine, theirs)):
        place = core if side == 0 else 1 - core
        for e in range(8):
            high, low, x = e >> 2, (e >> 1) & 1, e & 1
            part, quarter = high * 2 + x, low * 2 + place
            row = pl.multiple_of(quarter * ROWS + part * 32, 32)
            down[pl.ds(row, 32), :] = ref[e, :32, :].astype(F32)
            block = ref[e, 32:64, :].astype(F32)
            for f in range(8):
                span = pl.ds(pl.multiple_of(f * 512 + quarter * ROWS, ROWS), ROWS)
                up[part * 32 : (part + 1) * 32, span] = block[:, f * ROWS : (f + 1) * ROWS]
            if low == 0:
                row = pl.multiple_of(place * 64 + part * 16, 16)
                pair = ref[e, 64:80, :].astype(F32) + ref[e + 2, 64:80, :].astype(F32)
                out[pl.ds(row, 16), :] = pair
    for e in range(8):
        own = mine[e, 80:112, :].astype(F32)[:24]
        other = theirs[e, 80:112, :].astype(F32)[:24]
        pair = []
        for wide in (jnp.where(core == 0, own, other), jnp.where(core == 0, other, own)):
            pair.append(
                jnp.concatenate([wide[:, j * ROWS : (j + 1) * ROWS] for j in range(8)], axis=0)
            )
        for index, ref in enumerate((query, key, value)):
            rows = slice(index * HEAD, (index + 1) * HEAD)
            both = jnp.concatenate([pair[0][rows], pair[1][rows]], axis=0)
            ref[:, e * ROWS : (e + 1) * ROWS] = both.T


def call(kernel, outs, scratch, flops, moved, *operands):
    in_specs = [pl.BlockSpec(memory_space=pltpu.SMEM if operand.dtype == jnp.int32 else pltpu.VMEM) for operand in operands]
    return pl.pallas_call(
        kernel,
        out_shape=[jax.ShapeDtypeStruct(shape, dtype) for shape, dtype in outs],
        in_specs=in_specs,
        out_specs=[pl.BlockSpec(memory_space=pltpu.VMEM)] * len(outs),
        scratch_shapes=scratch,
        compiler_params=pltpu.CompilerParams(vmem_limit_bytes=VMEM_LIMIT),
        cost_estimate=pl.CostEstimate(flops=flops, bytes_accessed=moved, transcendentals=0),
    )(*operands)


def on_device(
    inputs,
    w_query,
    b_query,
    w_key,
    w_value,
    b_value,
    w_out,
    b_out,
    gain_one,
    shift_one,
    w_up,
    b_up,
    w_down,
    b_down,
    gain_two,
    shift_two,
    cotangent,
):
    ctx, fsdp = lax.axis_index("ctx"), lax.axis_index("fsdp")
    core = ctx & 1

    vectors = jnp.concatenate(
        [
            jnp.stack([b_query, b_value, b_out, gain_one, shift_one, b_down, gain_two, shift_two]),
            b_up.reshape(4, ROWS),
            jnp.zeros((4, ROWS), LOW),
        ]
    )
    at = ctx.reshape(1).astype(jnp.int32)
    (heads,) = call(
        pack_kernel,
        [((8, 208, ROWS), LOW)],
        [pltpu.VMEM((ROWS, ROWS), F32)],
        10**6,
        10**6,
        at,
        w_query,
        w_key,
        w_value,
        vectors,
    )
    own = after(inputs.reshape(ROWS, WIDTH), heads)
    heads = exchange(heads, "fsdp")
    pair = jnp.concatenate([own, swap(own, FAR_X)], axis=0)
    pair = after(pair, heads)
    parts = [pair] + [along_y(pair, k) for k in (1, 2, 3)]
    parts = parts + [swap(part, CORE) for part in parts]
    order = jnp.stack(
        [
            (((ctx >> 2) - k) % 4) * 4 + ((ctx & 3) ^ (2 * j + s))
            for s in range(2)
            for k in range(4)
            for j in range(2)
        ]
    ).astype(jnp.int32)

    early, late = call(
        weights_kernel,
        [((8, 240, WIDTH), LOW), ((8, 80, WIDTH), LOW)],
        [],
        10**6,
        10**7,
        at,
        w_out,
        w_up,
        w_down,
    )
    early = exchange(after(early, pair), "fsdp")
    vecs = heads[:, 3 * HEAD :, :].astype(F32)

    def whole(index):
        return vecs[:, index, :].reshape(WIDTH)

    vec_query, vec_value, vec_out, gain_a, shift_a, vec_down, gain_b, shift_b = (
        whole(index) for index in range(8)
    )
    quarter = ((ctx >> 2) & 1) * 2 + core
    vec_up = lax.dynamic_slice(vecs, (0, 8 + quarter, 0), (8, 1, ROWS)).reshape(WIDTH)
    bias_q = lax.dynamic_slice(vec_query, (ctx * HEAD,), (HEAD,)).reshape(HEAD, 1)
    bias_v = lax.dynamic_slice(vec_value, (ctx * HEAD,), (HEAD,)).reshape(HEAD, 1)

    def pick(block, index, axis):
        return lax.dynamic_index_in_dim(block, index, axis, keepdims=False)

    def by_core(mine, theirs, axis):
        first, second = jnp.where(core == 0, mine, theirs), jnp.where(core == 0, theirs, mine)
        return jnp.stack([first, second], axis=axis)

    qkv, rows, mixed_low, mixed, total, own_weight = call(
        forward_kernel,
        [
            ((3 * HEAD, LENGTH), LOW),
            ((LENGTH, 2 * HEAD), LOW),
            ((16, HEAD, ROWS), LOW),
            ((HEAD, LENGTH), F32),
            ((1, LENGTH), F32),
            ((3 * HEAD, WIDTH), LOW),
        ],
        [pltpu.VMEM((LENGTH, QUERIES), F32)],
        10**10,
        10**7,
        order,
        *parts,
        heads,
        bias_q,
        bias_v,
    )
    early, mixed_low = lax.optimization_barrier((early, mixed_low))
    context = exchange(mixed_low, "ctx")
    out_mine = early[:, :64].reshape(512, WIDTH)
    out_theirs = swap(out_mine, CORE)
    mat_up = early[:, 64 : 64 + ROWS].reshape(WIDTH, WIDTH)
    late = exchange(after(late, context), "fsdp")
    early_down = early[:, 64 + ROWS :]
    context_mine = pick(context.reshape(8, 2, HEAD, ROWS), core, 1).reshape(512, ROWS)
    context_theirs = pick(context.reshape(8, 2, HEAD, ROWS), 1 - core, 1).reshape(512, ROWS)
    context = context.reshape(WIDTH, ROWS)

    def share(block, ready=()):
        block = after(jnp.concatenate([block, swap(block, NEAR_Y)], axis=0), ready)
        return jnp.concatenate([block, swap(block, CORE)], axis=0)

    def collect(partial):
        half = partial[: 2 * ROWS] + swap(partial[2 * ROWS :].astype(LOW), CORE).astype(F32)
        return half[:ROWS] + swap(half[ROWS:].astype(LOW), NEAR_Y).astype(F32)

    branch = dims(context_mine, out_mine, 0, 0) + dims(context_theirs, out_theirs, 0, 0) + vec_out
    first, unit_one, scale_one = norm_forward(own.astype(F32) + branch, gain_a, shift_a)
    mat_up, early_down = lax.optimization_barrier((mat_up, early_down))
    first_all = share(first.astype(LOW), (mat_up, early_down))
    mat_down = jnp.concatenate([early_down, late], axis=1).reshape(WIDTH, WIDTH)
    hidden = dot(first_all, mat_up) + vec_up
    gate = 0.5 * (1.0 + lax.erf(hidden * (0.5**0.5)))
    slope = gate + hidden * jnp.exp(-0.5 * hidden * hidden) * 0.3989422804014327
    active = (hidden * gate).astype(LOW)
    second = collect(dot(active, mat_down)) + vec_down
    result, unit_two, scale_two = norm_forward(first + second, gain_b, shift_b)

    grad_out = cotangent.reshape(ROWS, WIDTH).astype(F32)
    grad_two, grad_gain_b, grad_shift_b = norm_backward(grad_out, unit_two, scale_two, gain_b)
    grad_second = grad_two.astype(LOW)
    grad_vec_down = jnp.sum(grad_second.astype(F32), axis=0)
    second_all = share(grad_second)
    down = dims(active, second_all, 0, 0).astype(LOW).reshape(4, 2, ROWS, WIDTH)
    z, low_x, low_y = fsdp >> 1, fsdp & 1, (ctx >> 2) & 1
    down_found = [along_z(pick(down, (z + k) % 4, 0), k) for k in (1, 3, 2)]
    grad_hidden = (slope * dims(second_all, mat_down, 1, 1)).astype(LOW)
    grad_vec_up = jnp.sum(grad_hidden.astype(F32), axis=0)
    up = dims(first_all, grad_hidden, 0, 0).astype(LOW).reshape(4, 2, ROWS, WIDTH)
    grad_first = grad_two + collect(dims(grad_hidden, mat_up, 1, 1))
    grad_first = after(grad_first, up)
    grad_one, grad_gain_a, grad_shift_a = norm_backward(grad_first, unit_one, scale_one, gain_a)
    grad_branch = after(grad_one.astype(LOW), down_found[:2])
    grad_vec_out = jnp.sum(grad_branch.astype(F32), axis=0)
    grad_context = by_core(
        dims(out_mine, grad_branch, 1, 1).reshape(8, HEAD, ROWS),
        dims(out_theirs, grad_branch, 1, 1).reshape(8, HEAD, ROWS),
        1,
    )
    grad_context = grad_context.astype(LOW).reshape(16, HEAD, ROWS)
    grad_heads = exchange(grad_context, "ctx")
    out = dot(after(context, grad_context), grad_branch).astype(LOW).reshape(8, 2, 64, WIDTH)
    out = pick(out, core, 1).astype(F32) + swap(pick(out, 1 - core, 1), CORE).astype(F32)
    sums = jnp.stack(
        [
            grad_vec_out,
            grad_gain_a,
            grad_shift_a,
            grad_vec_down,
            grad_gain_b,
            grad_shift_b,
            grad_vec_up,
            jnp.zeros_like(grad_vec_up),
        ]
    )
    sums = sums.reshape(8, 4, 2, ROWS).transpose(1, 2, 0, 3).reshape(4, 2, WIDTH)
    sums = jnp.concatenate([sums, jnp.zeros((4, 6, WIDTH), F32)], axis=1)
    (quarter_message,) = call(
        quarter_kernel, [((4, 144, WIDTH), LOW)], [], 10**6, 10**6, out, sums
    )
    summed = exchange(after(quarter_message, grad_heads), "ctx", SAME_QUARTER)
    grad_heads = after(grad_heads, quarter_message)
    message, *shares = call(
        backward_kernel,
        [((8, 32, WIDTH), LOW)] + [((QUERIES, WIDTH), LOW)] * 8,
        [pltpu.VMEM((3 * HEAD, LENGTH), LOW), pltpu.VMEM((HEAD, LENGTH), F32), pltpu.VMEM((HEAD, LENGTH), F32)],
        10**6,
        10**5,
        order,
        grad_heads,
        qkv,
        rows,
        mixed,
        total,
        *parts,
        own_weight,
    )
    up = after(up, quarter_message)
    up_found = [along_z(pick(up, (z + k) % 4, 0), k) for k in (1, 3, 2)]
    down_found = after([*down_found[:2], after(down_found[2], grad_context)], message)
    theirs = [swap(share, CORE) for share in shares[4:]]
    message = after(message, up_found)
    (message,) = call(
        extra_kernel, [((8, 64, WIDTH), LOW)], [], 10**6, 10**6, at, summed, message
    )
    shares, theirs = after((shares, theirs), message)
    def own_sum(blocks, found):
        total = pick(blocks, z, 0).astype(F32)
        for part in found:
            total += part.astype(F32)
        return pick(total, low_x, 0), along_x(pick(total, 1 - low_x, 0).astype(LOW))

    down, down_found = own_sum(down, down_found)
    down += after(down_found, message).astype(F32)
    up, up_found = own_sum(up, after(up_found, message))
    up += up_found.astype(F32)

    summed = jnp.sum(exchange(message, "fsdp").astype(F32), axis=0)

    shares = [mine.astype(F32) + other.astype(F32) for mine, other in zip(shares[:4], theirs)]
    pair, sent = shares[0], [share.astype(LOW) for share in shares[1:]]
    found = [along_y(sent[k - 1], -k) for k in (1, 3, 2)]

    hidden_rows = jnp.concatenate(
        [down.reshape(4, 32, WIDTH).astype(LOW), up.reshape(4, 32, WIDTH).astype(LOW)], axis=1
    )
    hidden_rows = after(hidden_rows, summed)
    found = after(found, hidden_rows)
    for part in found:
        pair += part.astype(F32)
    grad_in = grad_one + pair[:ROWS] + swap(pair[ROWS:].astype(LOW), FAR_X).astype(F32)
    hidden_rows = exchange(hidden_rows, "ctx", SAME_QUARTER)
    hidden_rows = jnp.sum(hidden_rows.astype(F32), axis=0)
    head_sums = summed[24:25, :512]
    head_sums = head_sums[:, :256] + head_sums[:, 256:]
    head_sums = jnp.concatenate([head_sums, jnp.zeros((1, 768), F32)], axis=1)

    message = jnp.concatenate(
        [
            hidden_rows.astype(LOW),
            summed[32:48].astype(LOW),
            summed[:24].astype(LOW),
            *split_low(head_sums),
            *split_low(summed[48:49] + summed[49:50]),
            jnp.zeros((4, WIDTH), LOW),
        ],
        axis=0,
    )
    message = after(message, pair)
    shared = exchange(repeated(message, 8), "ctx", SAME_CORE)
    shared = after(shared, grad_in)
    shared_theirs = swap(shared, CORE)
    square = ((ROWS, WIDTH), F32)
    grad_mat_down, grad_mat_up, grad_mat_out, grad_mat_query, grad_mat_key, grad_mat_value = call(
        assembly_kernel,
        [((512, WIDTH), F32), ((ROWS, 4096), F32), square, square, square, square],
        [],
        10**6,
        10**7,
        at,
        shared,
        shared_theirs,
    )

    def joined(block):
        return block[0].astype(F32) + block[1].astype(F32)

    holder = (z >> 1) * 4 + (z & 1)
    sums = jnp.stack([joined(pick(shared, holder + e, 0)[106:108]) for e in (0, 2)])
    sums_theirs = jnp.stack([joined(pick(shared_theirs, holder + e, 0)[106:108]) for e in (0, 2)])
    sums = by_core(sums, sums_theirs, 1).reshape(4, 8, ROWS)
    grad_vec_up = sums[:, 6].reshape(512)
    vector_grads = jnp.sum(sums[:, :6], axis=0)
    head_sums = by_core(pick(shared, fsdp, 0)[104:106], pick(shared_theirs, fsdp, 0)[104:106], 0)
    head_sums = (head_sums[:, 0].astype(F32) + head_sums[:, 1].astype(F32)).reshape(2, 8, ROWS)
    grad_vec_query = head_sums[:, 0, :HEAD].reshape(ROWS)
    grad_vec_value = head_sums[:, 1, :HEAD].reshape(ROWS)

    return (
        result.reshape(1, ROWS, WIDTH).astype(LOW),
        grad_in.reshape(1, ROWS, WIDTH),
        grad_mat_query,
        grad_vec_query,
        grad_mat_key,
        grad_mat_value,
        grad_vec_value,
        grad_mat_out,
        vector_grads[0],
        vector_grads[1],
        vector_grads[2],
        grad_mat_up,
        grad_vec_up,
        grad_mat_down,
        vector_grads[3],
        vector_grads[4],
        vector_grads[5],
    )


def solution(mesh):
    tokens, matrix, vector = P("fsdp", "ctx", None), P("fsdp", None), P("fsdp")
    return jax.shard_map(
        on_device,
        mesh=mesh,
        in_specs=(
            tokens,
            matrix,
            vector,
            matrix,
            matrix,
            vector,
            matrix,
            vector,
            vector,
            vector,
            matrix,
            vector,
            matrix,
            vector,
            vector,
            vector,
            tokens,
        ),
        out_specs=(
            tokens,
            tokens,
            matrix,
            vector,
            matrix,
            matrix,
            vector,
            matrix,
            vector,
            vector,
            vector,
            matrix,
            vector,
            matrix,
            vector,
            vector,
            vector,
        ),
        check_vma=False,
    )
```
